32 devices in a mesh: group: 2 (over x), gz: 16 (over z, y, core).
Axes of the slice: x: 2, y: 2, z: 4, core: 2. Of those that a mesh axis runs over, the one named last changes fastest.
Arguments:
- velocity: float32 [2, 3, 32, 256, 256], P('group', None, 'gz'), may hold values from -5 to 5
- fringe_start: int32 [1], replicated, may hold values from 0 to 224
- turbine_level: int32 [64], replicated, may hold values from 0 to 31
- turbine_row: int32 [64], replicated, may hold values from 0 to 255
- turbine_col: int32 [64], replicated, may hold values from 0 to 255
- thrust: float32 [64], replicated, may hold values from 1 to 12
- green_basis: float32 [32, 32], replicated, may hold values from -0.5 to 2.5
- eigen_shift: float32 [32], replicated, may hold values from 0.05 to 1
Outputs:
- updated: float32 [2, 3, 32, 256, 256], P('group', None, 'gz')
- pressure: float32 [2, 32, 256, 256], P('group', 'gz')
The draws below stay inside these ranges and needn't reach their ends.
All inputs are finite; a program needn't handle non-finite values.
Results may differ from the reference program's by a relative error of at most 0.00011.
Values sent between devices are 32-bit elements; how exact they have to be, the bound alone decides.
A program may use at most 64 MiB of HBM per device.

```python
import math
import jax
import jax.numpy as jnp
from jax import lax

NY = 256
NX = 256
TURB = 64
FRINGE = 32
NZ = 32
MEMBERS = 2


def draw_green_basis(key, part):
    noise = jax.random.normal(jax.random.fold_in(key, 7), (NZ, NZ), jnp.float32) * (0.8 / math.sqrt(NZ))
    noise = jnp.clip(noise, -0.5, 0.5)
    leading = 2.0
    return leading * jnp.eye(NZ, dtype=jnp.float32) + noise


def with_ends(result, rng, least, high):
    index_at = [jax.random.randint(jax.random.fold_in(rng, axis), (), 0, length) for axis, length in enumerate(result.shape)]
    widest = result.shape.index(max(result.shape))
    beside = index_at[:widest] + [(index_at[widest] + 1) % result.shape[widest]] + index_at[widest + 1:]
    return result.at[tuple(index_at)].set(least).at[tuple(beside)].set(high)


def steps_of(own_key, dims, split, low, top_value):
    def one(position, shards_of):
        heights = jax.random.uniform(jax.random.fold_in(jax.random.fold_in(own_key, 6), position), (shards_of,), jnp.float32, low / len(split), top_value / len(split))
        return jnp.repeat(jnp.exp(heights), dims[position] // shards_of).reshape((-1,) + (1,) * (len(dims) - position - 1))

    loudness = one(*split[0])
    for cut in split[1:]:
        loudness = loudness * one(*cut)
    return loudness


def gaussian(key, dims, spread, most, shards=(), kind=jnp.bfloat16):
    values = jax.random.normal(key, dims, jnp.float32) * spread
    if len(shards) > 0:
        values = steps_of(key, dims, shards, -0.22, 0.18) * values
    return jnp.clip(values, min=-most, max=most).astype(kind)


def setup_inputs(seed: int = 0) -> dict:
    key_of = jax.random.split(jax.random.key(seed), 9)
    return {
        "velocity": gaussian(key_of[0], (MEMBERS, 3, NZ, NY, NX), 1.0, 5.0, ((0, 2), (2, 16)), jnp.float32),
        "fringe_start": jax.random.randint(key_of[1], (1,), 0, NX - FRINGE + 1).astype(jnp.int32),
        "turbine_level": with_ends(jax.random.randint(key_of[2], (TURB,), 0, NZ), jax.random.fold_in(key_of[2], 1), 0, NZ - 1).astype(jnp.int32),
        "turbine_row": with_ends(jax.random.randint(key_of[3], (TURB,), 0, NY), jax.random.fold_in(key_of[3], 1), 0, NY - 1).astype(jnp.int32),
        "turbine_col": with_ends(jax.random.randint(key_of[4], (TURB,), 0, NX), jax.random.fold_in(key_of[4], 1), 0, NX - 1).astype(jnp.int32),
        "thrust": jnp.clip(jnp.exp(jax.random.uniform(key_of[5], (TURB,), jnp.float32, math.log(1.0), math.log(12.0))), 1.0, 12.0),
        "green_basis": draw_green_basis(jax.random.fold_in(key_of[8], 71), 0),
        "eigen_shift": jnp.clip(jnp.exp(jax.random.uniform(key_of[7], (NZ,), jnp.float32, math.log(0.05), math.log(1.0))), 0.05, 1.0),
    }


highest = lax.Precision.HIGHEST
time_step = 0.25

def wavenumber(ids, length):
    middle = length // 2
    return jnp.where(ids <= middle, ids, ids - middle)

def real_basis(length):
    row_ids = jnp.arange(length, dtype=jnp.int32)[:, None]
    col_ids = jnp.arange(length, dtype=jnp.int32)[None, :]
    middle = length // 2
    phases = 2.0 * jnp.pi / length * (wavenumber(row_ids, length) * col_ids % length).astype(jnp.float32)
    edges = (row_ids == 0) | (row_ids == middle)
    weights_norm = jnp.sqrt(jnp.where(edges, 1.0, 2.0) / length)
    return (jnp.where(row_ids <= middle, jnp.cos(phases), jnp.sin(phases)) * weights_norm).astype(jnp.float32)

def derivative(length):
    row_ids = jnp.arange(length, dtype=jnp.int32)[:, None]
    col_ids = jnp.arange(length, dtype=jnp.int32)[None, :]
    middle = length // 2
    omega_upper = 2.0 * jnp.pi / length * row_ids.astype(jnp.float32)
    omega_lower = 2.0 * jnp.pi / length * (row_ids - middle).astype(jnp.float32)
    upper = jnp.where((row_ids >= 1) & (row_ids < middle) & (col_ids == row_ids + middle), omega_upper, 0.0)
    lower = jnp.where((row_ids > middle) & (col_ids == row_ids - middle), -omega_lower, 0.0)
    basis = real_basis(length)
    return jnp.dot(basis.T, jnp.dot(upper + lower, basis, precision=highest), precision=highest)

def wave_square(ids, length):
    wave = wavenumber(ids, length).astype(jnp.float32) * (2.0 * jnp.pi / length)
    return wave * wave

def x_derivative(field, matrix):
    return jnp.einsum('...yb,ab->...ya', field, matrix, precision=highest)

def y_derivative(field, matrix):
    return jnp.einsum('ab,...bx->...ax', matrix, field, precision=highest)

def forward_plane(field, basis_y, basis_x):
    return x_derivative(y_derivative(field, basis_y), basis_x)

def inverse_plane(field, basis_y, basis_x):
    return x_derivative(y_derivative(field, basis_y.T), basis_x.T)

def advection(fields, vertical, deriv_y, deriv_x):
    along_x = x_derivative(fields, deriv_x)
    along_y = y_derivative(fields, deriv_y)
    return -(fields[0:1] * along_x + fields[1:2] * along_y + fields[2:3] * vertical)

def fringe_shape(offset):
    sine_part = jnp.sin(jnp.pi * (offset + 0.5) / FRINGE)
    return sine_part * sine_part

def reference(velocity, fringe_start, turbine_level, turbine_row, turbine_col, thrust, green_basis, eigen_shift):
    basis_y = real_basis(NY)
    basis_x = real_basis(NX)
    deriv_y = derivative(NY)
    deriv_x = derivative(NX)
    modes_ksq = (wave_square(jnp.arange(NY, dtype=jnp.int32)[:, None], NY) + wave_square(jnp.arange(NX, dtype=jnp.int32)[None, :], NX)).reshape(NY * NX)
    offset = jnp.arange(NX, dtype=jnp.int32) - fringe_start[0]
    inside = (offset >= 0) & (offset < FRINGE)
    fringe_ramp = jnp.where(inside, fringe_shape(offset.astype(jnp.float32)), 0.0)
    results = []
    pressures = []
    for member in range(MEMBERS):
        fields = velocity[member]
        is_farm = 1.0 if member > 0 else 0.0
        padded = jnp.pad(fields, ((0, 0), (1, 1), (0, 0), (0, 0)))
        vertical = 0.5 * (padded[:, 2:] - padded[:, :-2])
        tendency = advection(fields, vertical, deriv_y, deriv_x)
        speed = fields[0]
        cell_speed = speed[turbine_level, turbine_row, turbine_col]
        drag_force = -thrust * jnp.abs(cell_speed) * cell_speed
        placed = jnp.zeros_like(speed).at[turbine_level, turbine_row, turbine_col].add(drag_force)
        tendency = jnp.concatenate([tendency[0:1] + is_farm * placed[None], tendency[1:]], 0)
        predicted = fields + time_step * tendency
        horizontal = predicted[:2] + is_farm * fringe_ramp * (velocity[0, :2] - predicted[:2])
        upward = predicted[2]
        below = jnp.concatenate([jnp.zeros((1, NY, NX), jnp.float32), upward[:-1]], 0)
        divergence = x_derivative(horizontal[0], deriv_x) + y_derivative(horizontal[1], deriv_y) + (upward - below)
        spectrum = forward_plane(divergence, basis_y, basis_x).reshape(NZ, NY * NX)
        scaled = jnp.dot(green_basis, spectrum, precision=highest) / (eigen_shift[:, None] + modes_ksq[None, :])
        pressure_modes = jnp.dot(green_basis.T, scaled, precision=highest)
        rise_modes = jnp.concatenate([pressure_modes[1:], jnp.zeros((1, NY * NX), jnp.float32)], 0) - pressure_modes
        pressure = inverse_plane(pressure_modes.reshape(NZ, NY, NX), basis_y, basis_x)
        rise = inverse_plane(rise_modes.reshape(NZ, NY, NX), basis_y, basis_x)
        correction = jnp.stack([x_derivative(pressure, deriv_x), y_derivative(pressure, deriv_y), rise], 0)
        results.append(jnp.concatenate([horizontal, upward[None]], 0) - correction)
        pressures.append(pressure)
    return (jnp.stack(results, 0), jnp.stack(pressures, 0))
```

```python
import functools

import jax
import jax.numpy as jnp
import numpy as np
from jax import lax
from jax.experimental import pallas as pl
from jax.experimental.pallas import tpu as pltpu
from jax.sharding import PartitionSpec as P

FRINGE = 32
TIME_STEP = 0.25
MESH = pl.DeviceIdType.MESH
F32 = jnp.float32
BF16 = jnp.bfloat16


def tables(length):
    ids = np.arange(length)
    middle = length // 2
    wave = np.where(ids <= middle, ids, ids - middle)
    phases = 2.0 * np.pi / length * ((wave[:, None] * ids[None, :]) % length)
    norm = np.sqrt(np.where((ids == 0) | (ids == middle), 1.0, 2.0) / length)[:, None]
    basis = np.where(ids[:, None] <= middle, np.cos(phases), np.sin(phases)) * norm
    coupling = np.zeros((length, length))
    inner = np.arange(1, middle)
    coupling[inner, inner + middle] = 2.0 * np.pi * inner / length
    coupling[inner + middle, inner] = -2.0 * np.pi * inner / length
    deriv = basis.T @ coupling @ basis
    deriv = 0.5 * (deriv - deriv.T)
    parts = []
    for matrix in (basis, basis.T, deriv):
        whole = matrix.astype(np.float32)
        high = whole.astype(jnp.bfloat16)
        parts += [high, (whole - high.astype(np.float32)).astype(jnp.bfloat16)]
    return np.stack(parts)


def split(value):
    high = value.astype(BF16)
    return high, (value - high.astype(F32)).astype(BF16)


def dot(left, right):
    return jnp.dot(left, right, preferred_element_type=F32)


def dot_nt(left, right):
    return lax.dot_general(left, right, (((1,), (1,)), ((), ())), preferred_element_type=F32)


def left_mul(high, low, value):
    vh, vl = split(value)
    return dot(jnp.concatenate([high, high, low], 1), jnp.concatenate([vh, vl, vh], 0))


def right_mul(value, high, low):
    vh, vl = split(value)
    return dot(jnp.concatenate([vh, vl, vh], 1), jnp.concatenate([high, high, low], 0))


def iota(shape, dim):
    return lax.broadcasted_iota(jnp.int32, shape, dim)


def onehot(hit):
    return jnp.where(hit, 1.0, 0.0).astype(BF16)


def kernel(
    n, groups,
    vel, start_ref, tlevel, trow, tcol, thrust, green, shift, ramp_tab, tab_y, tab_x,
    upd, prs,
    below, above, fr_src, fr_buf, p_above,
    spec, modes, back, planes, m_hi, m_lo, mt_hi, mt_lo, inv,
    halo_send, halo_recv, fr_send, fr_recv, pa_send, pa_recv, x_send, x_recv, y_send, y_recv,
):
    levels, ny, nx = vel.shape[1:]
    rows = ny // n
    nz = levels * n
    nb = nz * rows
    me = lax.axis_index("gz")
    group = lax.axis_index("group")
    up = lax.rem(me + 1, n)
    down = lax.rem(me + n - 1, n)
    top = levels - 1
    has_up = me < n - 1
    has_down = me > 0

    barrier = pltpu.get_barrier_semaphore()

    @pl.loop(1, n)
    def _(off):
        pl.semaphore_signal(
            barrier, inc=1, device_id={"gz": lax.rem(me + off, n)}, device_id_type=MESH
        )

    for off in range(1, groups):
        pl.semaphore_signal(
            barrier, inc=1, device_id={"group": lax.rem(group + off, groups)}, device_id_type=MESH
        )
    pl.semaphore_wait(barrier, n - 1 + groups - 1)

    def remote(src, dst, send, recv, where):
        return pltpu.make_async_remote_copy(
            src_ref=src, dst_ref=dst, send_sem=send, recv_sem=recv,
            device_id=where, device_id_type=MESH,
        )

    w_up = remote(vel.at[2, top], below.at[2], halo_send.at[0], halo_recv.at[0], {"gz": up})
    all_down = remote(vel.at[:, 0], above, halo_send.at[1], halo_recv.at[1], {"gz": down})
    uv_up = remote(
        vel.at[pl.ds(0, 2), top], below.at[pl.ds(0, 2)], halo_send.at[2], halo_recv.at[2],
        {"gz": up},
    )
    w2_up = remote(vel.at[2, top - 1], below.at[3], halo_send.at[3], halo_recv.at[3], {"gz": up})

    @pl.when(has_up)
    def _():
        w_up.start()

    @pl.when(has_down)
    def _():
        all_down.start()

    @pl.when(has_up)
    def _():
        uv_up.start()
        w2_up.start()

    @pl.when(jnp.logical_not(has_down))
    def _():
        below[...] = jnp.zeros_like(below)

    @pl.when(jnp.logical_not(has_up))
    def _():
        above[...] = jnp.zeros_like(above)
        p_above[...] = jnp.zeros_like(p_above)

    start = start_ref[0]
    pick = iota((FRINGE, nx), 1) - start == iota((FRINGE, nx), 0)
    pick_b = onehot(pick)
    fringe_copies = [
        remote(fr_src, fr_buf, fr_send.at[g - 1], fr_recv, {"group": g}) for g in range(1, groups)
    ]

    @pl.when(group == 0)
    def _():
        fr_buf[...] = jnp.zeros_like(fr_buf)
        for c in range(2):
            for k in range(levels):
                vh, vl = split(vel[c, k])
                fr_src[c * levels + k] = dot_nt(pick_b, vh) + dot_nt(pick_b, vl)
        for copy in fringe_copies:
            copy.start()

    is_farm = jnp.where(group > 0, 1.0, 0.0)
    ramp = is_farm * jnp.sum(jnp.where(pick, ramp_tab[...], 0.0), axis=0, keepdims=True)

    r_y = (tab_y[0], tab_y[1])
    rt_y = (tab_y[2], tab_y[3])
    d_y = (tab_y[4], tab_y[5])
    r_x = (tab_x[0], tab_x[1])
    rt_x = (tab_x[2], tab_x[3])
    d_x = (tab_x[4], tab_x[5])

    def dx(value):
        return -right_mul(value, *d_x)

    def dy(value):
        return left_mul(*d_y, value)

    turbines = trow.shape[1]
    pick_row = iota((ny, turbines), 0) == trow[...]
    pick_col = onehot(iota((nx, turbines), 0) == tcol[...])
    speed = jnp.zeros((1, turbines), F32)
    for k in range(levels):
        vh, vl = split(vel[0, k])
        at_col = dot(vh, pick_col) + dot(vl, pick_col)
        here = jnp.sum(jnp.where(pick_row, at_col, 0.0), axis=0, keepdims=True)
        speed = speed + jnp.where(tlevel[...] == me * levels + k, here, 0.0)
    drag = -is_farm * thrust[...] * jnp.abs(speed) * speed
    for k in range(levels):
        for c in range(3):
            field = vel[c, k]
            if k < top and k > 0:
                vertical = vel[c, k + 1] - vel[c, k - 1]
            elif k < top:
                vertical = vel[c, k + 1]
            elif k > 0:
                vertical = -vel[c, k - 1]
            else:
                vertical = jnp.zeros_like(field)
            tend = -(
                vel[0, k] * dx(field) + vel[1, k] * dy(field) + (0.5 * vel[2, k]) * vertical
            )
            if c == 0:
                placed = jnp.where(
                    pick_row & (tlevel[...] == me * levels + k), drag, 0.0
                )
                ph, pw = split(placed)
                tend = tend + dot_nt(ph, pick_col) + dot_nt(pw, pick_col)
            upd[c, k] = field + TIME_STEP * tend

    rbits = rows.bit_length() - 1
    ybits = ny.bit_length() - 1
    eig = iota((nb, nz), 0) >> rbits == iota((nb, nz), 1)
    pos = iota((nb, nz), 0)
    lev = ((pos & (ny - 1)) >> rbits) * levels + (pos >> ybits) == iota((nb, nz), 1)
    eig_b, lev_b = onehot(eig), onehot(lev)
    same = (iota((nb, nb), 0) & (rows - 1)) == (iota((nb, nb), 1) & (rows - 1))
    for part, to, to_t in zip(split(green[...]), (m_hi, m_lo), (mt_hi, mt_lo)):
        wide = dot(eig_b, part).astype(BF16)
        to[...] = jnp.where(same, dot_nt(wide, lev_b), 0.0).astype(BF16)
        wide_t = dot_nt(lev_b, part).astype(BF16)
        to_t[...] = jnp.where(same, dot_nt(wide_t, eig_b), 0.0).astype(BF16)
    shifts = jnp.sum(jnp.where(eig, shift[...], 0.0), axis=1, keepdims=True)

    def wave_square(ids, length):
        wave = jnp.where(ids <= length // 2, ids, ids - length // 2)
        wave = wave.astype(F32) * (2.0 * np.pi / length)
        return wave * wave

    ky = me * rows + (iota((nb, 1), 0) & (rows - 1))
    kx = iota((1, nx), 1)
    inv[...] = 1.0 / (shifts + (wave_square(ky, ny) + wave_square(kx, nx)))

    def put(ref, value):
        if rows % 8 == 0:
            ref[...] = value.reshape(n, rows, nx)
        else:
            for i in range(n):
                ref[i] = value[i * rows : (i + 1) * rows]

    def get(ref):
        if rows % 8 == 0:
            return ref[...].reshape(ny, nx)
        return jnp.concatenate([ref[i] for i in range(n)], 0)

    def exchange(src, dst, send, recv):
        pltpu.make_async_copy(src.at[me], dst.at[me], recv).start()

        @pl.loop(1, n)
        def _(off):
            peer = lax.rem(me + off, n)
            remote(src.at[peer], dst.at[me], send, recv, {"gz": peer}).start()

    def arrived(dst, recv):
        pltpu.make_async_copy(dst, dst, recv).wait()

    def sent(src, send):
        most = src.at[pl.ds(0, n - 1)]
        pltpu.make_async_copy(most, most, send).wait()

    @pl.when(group > 0)
    def _():
        fringe_copies[0].wait_recv()

    def blend(c, k, predicted):
        th, tl = split(fr_buf[c * levels + k].T)
        upstream = dot(th, pick_b) + dot(tl, pick_b)
        return predicted + ramp * (upstream - predicted)

    def transform(k, under):
        divergence = dx(upd[0, k]) + dy(upd[1, k]) + (upd[2, k] - under)
        put(spec.at[k], right_mul(left_mul(*r_y, divergence), *rt_x))
        exchange(spec.at[k], modes.at[k], x_send.at[k], x_recv.at[k])

    half = 0.5 * TIME_STEP

    @pl.when(has_up)
    def _():
        all_down.wait_recv()

    for c in range(3):
        upd[c, top] = upd[c, top] - half * vel[2, top] * above[c]

    @pl.when(has_down)
    def _():
        w_up.wait_recv()

    upd[2, 0] = upd[2, 0] + half * vel[2, 0] * below[2]
    for k in range(top, 0, -1):
        for c in range(2):
            upd[c, k] = blend(c, k, upd[c, k])
        transform(k, upd[2, k - 1])

    @pl.when(has_down)
    def _():
        uv_up.wait_recv()
        w2_up.wait_recv()

    for c in range(2):
        upd[c, 0] = blend(c, 0, upd[c, 0] + half * vel[2, 0] * below[c])
    w_ghost = below[2]
    ghost = w_ghost - TIME_STEP * (
        below[0] * dx(w_ghost)
        + below[1] * dy(w_ghost)
        + (0.5 * w_ghost) * (vel[2, 0] - below[3])
    )
    transform(0, ghost)

    scaled = None
    for k in range(top, -1, -1):
        arrived(modes.at[k], x_recv.at[k])
        cols = pl.ds(k * ny, ny)
        term = left_mul(m_hi[:, cols], m_lo[:, cols], get(modes.at[k]))
        scaled = term if scaled is None else scaled + term
    scaled = scaled * inv[...]
    for k in range(levels):
        own = pl.ds(k * ny, ny)
        put(back.at[k], left_mul(mt_hi[own], mt_lo[own], scaled))
        exchange(back.at[k], planes.at[k], y_send.at[k], y_recv.at[k])

    p_down = remote(prs.at[0], p_above, pa_send, pa_recv, {"gz": down})
    for k in range(levels):
        arrived(planes.at[k], y_recv.at[k])
        pressure = right_mul(left_mul(*rt_y, get(planes.at[k])), *r_x)
        prs[k] = pressure
        if k == 0:

            @pl.when(has_down)
            def _():
                p_down.start()

        else:
            upd[2, k - 1] = upd[2, k - 1] - (pressure - prs[k - 1])
        upd[0, k] = upd[0, k] - dx(pressure)
        upd[1, k] = upd[1, k] - dy(pressure)

    @pl.when(has_up)
    def _():
        p_down.wait_recv()

    upd[2, top] = upd[2, top] - (p_above[...] - prs[top])

    @pl.when(has_up)
    def _():
        w_up.wait_send()
        uv_up.wait_send()
        w2_up.wait_send()

    @pl.when(has_down)
    def _():
        all_down.wait_send()
        p_down.wait_send()

    @pl.when(group == 0)
    def _():
        for copy in fringe_copies:
            copy.wait_send()

    for k in range(levels):
        sent(spec.at[k], x_send.at[k])
        sent(back.at[k], y_send.at[k])


def local(
    n, groups,
    velocity, fringe_start, turbine_level, turbine_row, turbine_col, thrust, green_basis,
    eigen_shift,
):
    _, _, levels, ny, nx = velocity.shape
    rows = ny // n
    nz = levels * n
    nb = nz * rows
    offset = (np.arange(FRINGE) + 0.5)[:, None]
    ramp_tab = (np.sin(np.pi * offset / FRINGE) ** 2).astype(np.float32)
    vmem = pl.BlockSpec(memory_space=pltpu.VMEM)
    smem = pl.BlockSpec(memory_space=pltpu.SMEM)
    plane = (n, rows, nx)
    dma = pltpu.SemaphoreType.DMA
    updated, pressure = pl.pallas_call(
        functools.partial(kernel, n, groups),
        out_shape=(
            jax.ShapeDtypeStruct((3, levels, ny, nx), F32),
            jax.ShapeDtypeStruct((levels, ny, nx), F32),
        ),
        in_specs=[vmem, smem] + [vmem] * 9,
        out_specs=(vmem, vmem),
        scratch_shapes=[
            pltpu.VMEM((4, ny, nx), F32),
            pltpu.VMEM((3, ny, nx), F32),
            pltpu.VMEM((2 * levels, FRINGE, ny), F32),
            pltpu.VMEM((2 * levels, FRINGE, ny), F32),
            pltpu.VMEM((ny, nx), F32),
            pltpu.VMEM((levels, *plane), F32),
            pltpu.VMEM((levels, *plane), F32),
            pltpu.VMEM((levels, *plane), F32),
            pltpu.VMEM((levels, *plane), F32),
            pltpu.VMEM((nb, nb), BF16),
            pltpu.VMEM((nb, nb), BF16),
            pltpu.VMEM((nb, nb), BF16),
            pltpu.VMEM((nb, nb), BF16),
            pltpu.VMEM((nb, nx), F32),
            dma((4,)),
            dma((4,)),
            dma((max(groups - 1, 1),)),
            dma,
            dma,
            dma,
            dma((levels,)),
            dma((levels,)),
            dma((levels,)),
            dma((levels,)),
        ],
        compiler_params=pltpu.CompilerParams(
            collective_id=0, has_side_effects=True, vmem_limit_bytes=44 * 1024 * 1024
        ),
        name="fractional_step",
    )(
        velocity[0], fringe_start,
        turbine_level[None], turbine_row[None], turbine_col[None], thrust[None],
        green_basis, eigen_shift[None], ramp_tab, tables(ny), tables(nx),
    )
    return updated[None], pressure[None]


def solution(mesh):
    return jax.shard_map(
        functools.partial(local, mesh.shape["gz"], mesh.shape["group"]),
        mesh=mesh,
        in_specs=(P("group", None, "gz", None, None), P(), P(), P(), P(), P(), P(), P()),
        out_specs=(P("group", None, "gz", None, None), P("group", "gz", None, None)),
        check_vma=False,
    )
```

```python
import functools

import jax
import jax.numpy as jnp
import numpy as np
from jax import lax
from jax.experimental import pallas as pl
from jax.experimental.pallas import tpu as pltpu
from jax.sharding import PartitionSpec as P

FRINGE = 32
TIME_STEP = 0.25
MESH = pl.DeviceIdType.MESH
F32 = jnp.float32
BF16 = jnp.bfloat16


def tables(length):
    ids = np.arange(length)
    middle = length // 2
    wave = np.where(ids <= middle, ids, ids - middle)
    phases = 2.0 * np.pi / length * ((wave[:, None] * ids[None, :]) % length)
    norm = np.sqrt(np.where((ids == 0) | (ids == middle), 1.0, 2.0) / length)[:, None]
    basis = np.where(ids[:, None] <= middle, np.cos(phases), np.sin(phases)) * norm
    coupling = np.zeros((length, length))
    inner = np.arange(1, middle)
    coupling[inner, inner + middle] = 2.0 * np.pi * inner / length
    coupling[inner + middle, inner] = -2.0 * np.pi * inner / length
    deriv = basis.T @ coupling @ basis
    deriv = 0.5 * (deriv - deriv.T)
    parts = []
    for matrix in (basis, basis.T, deriv):
        whole = matrix.astype(np.float32)
        high = whole.astype(jnp.bfloat16)
        parts += [high, (whole - high.astype(np.float32)).astype(jnp.bfloat16)]
    return np.stack(parts)


def split(value):
    high = value.astype(BF16)
    return high, (value - high.astype(F32)).astype(BF16)


def dot(left, right):
    return jnp.dot(left, right, preferred_element_type=F32)


def dot_nt(left, right):
    return lax.dot_general(left, right, (((1,), (1,)), ((), ())), preferred_element_type=F32)


def left_mul(high, low, value):
    vh, vl = split(value)
    return dot(jnp.concatenate([high, high, low], 1), jnp.concatenate([vh, vl, vh], 0))


def right_mul(value, high, low):
    vh, vl = split(value)
    return dot(jnp.concatenate([vh, vl, vh], 1), jnp.concatenate([high, high, low], 0))


def iota(shape, dim):
    return lax.broadcasted_iota(jnp.int32, shape, dim)


def onehot(hit):
    return jnp.where(hit, 1.0, 0.0).astype(BF16)


def kernel(
    n, groups, tab_count,
    vel_hbm, start_ref, *refs,
):
    staged = refs[: 7 + tab_count]
    upd_hbm, prs_hbm = refs[7 + tab_count : 9 + tab_count]
    vel = refs[9 + tab_count]
    local_refs = refs[10 + tab_count : 17 + 2 * tab_count]
    tlevel, trow, tcol, thrust, green, shift, ramp_tab = local_refs[:7]
    tab_y, tab_x = local_refs[7], local_refs[-1]
    (
        upd, prs, below, above, h_src, h_below, h_above, fr_src, fr_buf, p_above,
        spec, modes, back, planes, m_hi, m_lo, mt_hi, mt_lo, inv,
        in_sem, out_sem, halo_send, halo_recv, fr_send, fr_recv, pa_send, pa_recv,
        x_send, x_recv, y_send, y_recv,
    ) = refs[17 + 2 * tab_count :]
    levels, ny, nx = vel.shape[1:]
    rows = ny // n
    nz = levels * n
    nb = nz * rows
    me = lax.axis_index("gz")
    group = lax.axis_index("group")
    up = lax.rem(me + 1, n)
    down = lax.rem(me + n - 1, n)
    top = levels - 1
    has_up = me < n - 1
    has_down = me > 0

    loads = [
        pltpu.make_async_copy(src, dst, in_sem.at[i])
        for i, (src, dst) in enumerate(zip((vel_hbm, *staged), (vel, *local_refs)))
    ]
    for load in loads:
        load.start()

    barrier = pltpu.get_barrier_semaphore()

    @pl.loop(1, n)
    def _(off):
        pl.semaphore_signal(
            barrier, inc=1, device_id={"gz": lax.rem(me + off, n)}, device_id_type=MESH
        )

    for off in range(1, groups):
        pl.semaphore_signal(
            barrier, inc=1, device_id={"group": lax.rem(group + off, groups)}, device_id_type=MESH
        )
    pl.semaphore_wait(barrier, n - 1 + groups - 1)

    def remote(src, dst, send, recv, where):
        return pltpu.make_async_remote_copy(
            src_ref=src, dst_ref=dst, send_sem=send, recv_sem=recv,
            device_id=where, device_id_type=MESH,
        )

    def halo(src, dst, i, where):
        return remote(src, dst, halo_send.at[i], halo_recv.at[i], {"gz": where})

    uv = pl.ds(0, 2)
    w_up = halo(vel_hbm.at[2, top], below.at[2], 0, up)
    w_down = halo(vel_hbm.at[2, 0], above.at[2], 1, down)
    h_up = halo(h_src.at[0], h_below, 2, up)
    h_down = halo(h_src.at[1], h_above, 3, down)
    uv_up = halo(vel_hbm.at[uv, top], below.at[uv], 4, up)
    uv_down = halo(vel_hbm.at[uv, 0], above.at[uv], 5, down)

    def go_up(*copies):
        @pl.when(has_up)
        def _():
            for copy in copies:
                copy.start()

    def go_down(*copies):
        @pl.when(has_down)
        def _():
            for copy in copies:
                copy.start()

    def from_below(copy):
        @pl.when(has_down)
        def _():
            copy.wait_recv()

    def from_above(copy):
        @pl.when(has_up)
        def _():
            copy.wait_recv()

    go_up(w_up)
    go_down(w_down)

    @pl.when(jnp.logical_not(has_down))
    def _():
        below[...] = jnp.zeros_like(below)
        h_below[...] = jnp.zeros_like(h_below)

    @pl.when(jnp.logical_not(has_up))
    def _():
        above[...] = jnp.zeros_like(above)
        h_above[...] = jnp.zeros_like(h_above)
        p_above[...] = jnp.zeros_like(p_above)

    for load in loads:
        load.wait()

    start = start_ref[0]
    pick = iota((FRINGE, nx), 1) - start == iota((FRINGE, nx), 0)
    pick_b = onehot(pick)
    fringe_copies = [
        remote(fr_src, fr_buf, fr_send.at[g - 1], fr_recv, {"group": g}) for g in range(1, groups)
    ]

    @pl.when(group == 0)
    def _():
        fr_buf[...] = jnp.zeros_like(fr_buf)
        for c in range(2):
            for k in range(levels):
                vh, vl = split(vel[c, k])
                fr_src[c * levels + k] = dot_nt(pick_b, vh) + dot_nt(pick_b, vl)
        for copy in fringe_copies:
            copy.start()

    is_farm = jnp.where(group > 0, 1.0, 0.0)
    ramp = is_farm * jnp.sum(jnp.where(pick, ramp_tab[...], 0.0), axis=0, keepdims=True)
    keep = 1.0 - ramp

    r_y = (tab_y[0], tab_y[1])
    rt_y = (tab_y[2], tab_y[3])
    d_y = (tab_y[4], tab_y[5])
    r_x = (tab_x[0], tab_x[1])
    rt_x = (tab_x[2], tab_x[3])
    d_x = (tab_x[4], tab_x[5])

    def dx(value):
        return -right_mul(value, *d_x)

    def dy(value):
        return left_mul(*d_y, value)

    turbines = trow.shape[1]
    pick_row = iota((ny, turbines), 0) == trow[...]
    pick_col = onehot(iota((nx, turbines), 0) == tcol[...])

    def predict(c, k):
        field = vel[c, k]
        if k < top and k > 0:
            vertical = vel[c, k + 1] - vel[c, k - 1]
        elif k < top:
            vertical = vel[c, k + 1]
        elif k > 0:
            vertical = -vel[c, k - 1]
        else:
            vertical = jnp.zeros_like(field)
        tend = -(vel[0, k] * dx(field) + vel[1, k] * dy(field) + (0.5 * vel[2, k]) * vertical)
        upd[c, k] = field + TIME_STEP * tend

    for k in range(levels):
        predict(2, k)

    half = 0.5 * TIME_STEP

    from_above(w_down)
    upd[2, top] = upd[2, top] - half * vel[2, top] * above[2]
    weight = (half * keep) * above[2]
    h_src[0] = dx(weight * vel[0, top]) + dy(weight * vel[1, top]) - upd[2, top]
    go_up(h_up)
    from_below(w_up)
    weight = (-half * keep) * below[2]
    h_src[1] = dx(weight * vel[0, 0]) + dy(weight * vel[1, 0])
    go_down(h_down)
    upd[2, 0] = upd[2, 0] + half * vel[2, 0] * below[2]

    speed = jnp.zeros((1, turbines), F32)
    for k in range(levels):
        vh, vl = split(vel[0, k])
        at_col = dot(vh, pick_col) + dot(vl, pick_col)
        here = jnp.sum(jnp.where(pick_row, at_col, 0.0), axis=0, keepdims=True)
        speed = speed + jnp.where(tlevel[...] == me * levels + k, here, 0.0)
    drag = (-TIME_STEP * is_farm) * thrust[...] * jnp.abs(speed) * speed
    for k in range(levels):
        predict(0, k)
        placed = jnp.where(pick_row & (tlevel[...] == me * levels + k), drag, 0.0)
        ph, pw = split(placed)
        upd[0, k] = upd[0, k] + dot_nt(ph, pick_col) + dot_nt(pw, pick_col)
        predict(1, k)

    @pl.when(group > 0)
    def _():
        fringe_copies[0].wait_recv()

    for k in range(levels):
        for c in range(2):
            th, tl = split(fr_buf[c * levels + k].T)
            upstream = dot(th, pick_b) + dot(tl, pick_b)
            predicted = upd[c, k]
            upd[c, k] = predicted + ramp * (upstream - predicted)

    for k in range(levels):
        divergence = dx(upd[0, k]) + dy(upd[1, k]) + upd[2, k]
        if k > 0:
            divergence = divergence - upd[2, k - 1]
        prs[k] = divergence

    rbits = rows.bit_length() - 1
    ybits = ny.bit_length() - 1
    eig = iota((nb, nz), 0) >> rbits == iota((nb, nz), 1)
    pos = iota((nb, nz), 0)
    lev = ((pos & (ny - 1)) >> rbits) * levels + (pos >> ybits) == iota((nb, nz), 1)
    eig_b, lev_b = onehot(eig), onehot(lev)
    same = (iota((nb, nb), 0) & (rows - 1)) == (iota((nb, nb), 1) & (rows - 1))
    for part, to, to_t in zip(split(green[...]), (m_hi, m_lo), (mt_hi, mt_lo)):
        wide = dot(eig_b, part).astype(BF16)
        to[...] = jnp.where(same, dot_nt(wide, lev_b), 0.0).astype(BF16)
        wide_t = dot_nt(lev_b, part).astype(BF16)
        to_t[...] = jnp.where(same, dot_nt(wide_t, eig_b), 0.0).astype(BF16)
    shifts = jnp.sum(jnp.where(eig, shift[...], 0.0), axis=1, keepdims=True)

    def wave_square(ids, length):
        wave = jnp.where(ids <= length // 2, ids, ids - length // 2)
        wave = wave.astype(F32) * (2.0 * np.pi / length)
        return wave * wave

    ky = me * rows + (iota((nb, 1), 0) & (rows - 1))
    kx = iota((1, nx), 1)
    inv[...] = 1.0 / (shifts + (wave_square(ky, ny) + wave_square(kx, nx)))

    def exchange(src, dst, send, recv):
        pltpu.make_async_copy(src.at[me], dst.at[me], recv).start()

        @pl.loop(1, n)
        def _(off):
            peer = lax.rem(me + off, n)
            remote(src.at[peer], dst.at[me], send, recv, {"gz": peer}).start()

    def arrived(dst, recv):
        pltpu.make_async_copy(dst, dst, recv).wait()

    def sent(src, send):
        most = src.at[pl.ds(0, n - 1)]
        pltpu.make_async_copy(most, most, send).wait()

    def transform(k):
        put(spec.at[k], right_mul(left_mul(*r_y, prs[k]), *rt_x), n)
        exchange(spec.at[k], modes.at[k], x_send.at[k], x_recv.at[k])

    from_above(h_down)
    prs[top] = prs[top] + h_above[...]
    if top > 0:
        transform(top)
    for k in range(top - 1, 0, -1):
        transform(k)
    from_below(h_up)
    prs[0] = prs[0] + h_below[...]
    transform(0)
    go_up(uv_up)

    scaled = None
    for k in range(top, -1, -1):
        arrived(modes.at[k], x_recv.at[k])
        cols = pl.ds(k * ny, ny)
        term = left_mul(m_hi[:, cols], m_lo[:, cols], get(modes.at[k]))
        scaled = term if scaled is None else scaled + term
    scaled = scaled * inv[...]
    for k in range(levels):
        own = pl.ds(k * ny, ny)
        put(back.at[k], left_mul(mt_hi[own], mt_lo[own], scaled), n)
        exchange(back.at[k], planes.at[k], y_send.at[k], y_recv.at[k])
    go_down(uv_down)

    from_below(uv_up)
    for c in range(2):
        upd[c, 0] = upd[c, 0] + (half * keep) * (vel[2, 0] * below[c])

    p_down = remote(prs.at[0], p_above, pa_send, pa_recv, {"gz": down})
    outs = []

    def leave(src, dst):
        copy = pltpu.make_async_copy(src, dst, out_sem.at[len(outs)])
        copy.start()
        outs.append(copy)

    for k in range(levels):
        arrived(planes.at[k], y_recv.at[k])
        pressure = right_mul(left_mul(*rt_y, get(planes.at[k])), *r_x)
        prs[k] = pressure
        leave(prs.at[k], prs_hbm.at[k])
        if k == 0:
            go_down(p_down)
        else:
            upd[2, k - 1] = upd[2, k - 1] - (pressure - prs[k - 1])
            leave(upd.at[2, k - 1], upd_hbm.at[2, k - 1])
        if k == top:
            from_above(uv_down)
            for c in range(2):
                upd[c, top] = upd[c, top] - (half * keep) * (vel[2, top] * above[c])
        upd[0, k] = upd[0, k] - dx(pressure)
        upd[1, k] = upd[1, k] - dy(pressure)
        leave(upd.at[uv, k], upd_hbm.at[uv, k])
    from_above(p_down)
    upd[2, top] = upd[2, top] - (p_above[...] - prs[top])
    leave(upd.at[2, top], upd_hbm.at[2, top])

    @pl.when(has_up)
    def _():
        for copy in (w_up, h_up, uv_up):
            copy.wait_send()

    @pl.when(has_down)
    def _():
        for copy in (w_down, h_down, uv_down, p_down):
            copy.wait_send()

    @pl.when(group == 0)
    def _():
        for copy in fringe_copies:
            copy.wait_send()

    for k in range(levels):
        sent(spec.at[k], x_send.at[k])
        sent(back.at[k], y_send.at[k])
    for copy in outs:
        copy.wait()


def put(ref, value, n):
    rows = ref.shape[1]
    if rows % 8 == 0:
        ref[...] = value.reshape(ref.shape)
    else:
        for i in range(n):
            ref[i] = value[i * rows : (i + 1) * rows]


def get(ref):
    n, rows, nx = ref.shape
    if rows % 8 == 0:
        return ref[...].reshape(n * rows, nx)
    return jnp.concatenate([ref[i] for i in range(n)], 0)


def local(
    n, groups,
    velocity, fringe_start, turbine_level, turbine_row, turbine_col, thrust, green_basis,
    eigen_shift,
):
    _, _, levels, ny, nx = velocity.shape
    rows = ny // n
    nz = levels * n
    nb = nz * rows
    offset = (np.arange(FRINGE) + 0.5)[:, None]
    ramp_tab = (np.sin(np.pi * offset / FRINGE) ** 2).astype(np.float32)
    hbm = pl.BlockSpec(memory_space=pltpu.HBM)
    smem = pl.BlockSpec(memory_space=pltpu.SMEM)
    plane = (n, rows, nx)
    dma = pltpu.SemaphoreType.DMA
    tabs = [tables(length) for length in ((ny,) if ny == nx else (ny, nx))]
    staged = [
        turbine_level[None], turbine_row[None], turbine_col[None], thrust[None],
        green_basis, eigen_shift[None], ramp_tab, *tabs,
    ]
    fields = velocity[0]
    updated, pressure = pl.pallas_call(
        functools.partial(kernel, n, groups, len(tabs)),
        out_shape=(
            jax.ShapeDtypeStruct((3, levels, ny, nx), F32),
            jax.ShapeDtypeStruct((levels, ny, nx), F32),
        ),
        in_specs=[hbm, smem] + [hbm] * len(staged),
        out_specs=(hbm, hbm),
        scratch_shapes=[pltpu.VMEM(x.shape, x.dtype) for x in (fields, *staged)]
        + [
            pltpu.VMEM((3, levels, ny, nx), F32),
            pltpu.VMEM((levels, ny, nx), F32),
            pltpu.VMEM((3, ny, nx), F32),
            pltpu.VMEM((3, ny, nx), F32),
            pltpu.VMEM((2, ny, nx), F32),
            pltpu.VMEM((ny, nx), F32),
            pltpu.VMEM((ny, nx), F32),
            pltpu.VMEM((2 * levels, FRINGE, ny), F32),
            pltpu.VMEM((2 * levels, FRINGE, ny), F32),
            pltpu.VMEM((ny, nx), F32),
            pltpu.VMEM((levels, *plane), F32),
            pltpu.VMEM((levels, *plane), F32),
            pltpu.VMEM((levels, *plane), F32),
            pltpu.VMEM((levels, *plane), F32),
            pltpu.VMEM((nb, nb), BF16),
            pltpu.VMEM((nb, nb), BF16),
            pltpu.VMEM((nb, nb), BF16),
            pltpu.VMEM((nb, nb), BF16),
            pltpu.VMEM((nb, nx), F32),
            dma((1 + len(staged),)),
            dma((3 * levels,)),
            dma((6,)),
            dma((6,)),
            dma((max(groups - 1, 1),)),
            dma,
            dma,
            dma,
            dma((levels,)),
            dma((levels,)),
            dma((levels,)),
            dma((levels,)),
        ],
        compiler_params=pltpu.CompilerParams(
            collective_id=0, has_side_effects=True, vmem_limit_bytes=56 * 1024 * 1024
        ),
        name="fractional_step",
    )(fields, fringe_start, *staged)
    return updated[None], pressure[None]


def solution(mesh):
    return jax.shard_map(
        functools.partial(local, mesh.shape["gz"], mesh.shape["group"]),
        mesh=mesh,
        in_specs=(P("group", None, "gz", None, None), P(), P(), P(), P(), P(), P(), P()),
        out_specs=(P("group", None, "gz", None, None), P("group", "gz", None, None)),
        check_vma=False,
    )
```

```python
import functools

import jax
import jax.numpy as jnp
import numpy as np
from jax import lax
from jax.experimental import pallas as pl
from jax.experimental.pallas import tpu as pltpu
from jax.sharding import PartitionSpec as P

FRINGE = 32
TIME_STEP = 0.25
MESH = pl.DeviceIdType.MESH
F32 = jnp.float32
BF16 = jnp.bfloat16


def tables(length):
    ids = np.arange(length)
    middle = length // 2
    wave = np.where(ids <= middle, ids, ids - middle)
    phases = 2.0 * np.pi / length * ((wave[:, None] * ids[None, :]) % length)
    norm = np.sqrt(np.where((ids == 0) | (ids == middle), 1.0, 2.0) / length)[:, None]
    basis = np.where(ids[:, None] <= middle, np.cos(phases), np.sin(phases)) * norm
    coupling = np.zeros((length, length))
    inner = np.arange(1, middle)
    coupling[inner, inner + middle] = 2.0 * np.pi * inner / length
    coupling[inner + middle, inner] = -2.0 * np.pi * inner / length
    deriv = basis.T @ coupling @ basis
    deriv = 0.5 * (deriv - deriv.T)
    parts = []
    for matrix in (basis, basis.T, deriv):
        whole = matrix.astype(np.float32)
        high = whole.astype(jnp.bfloat16)
        parts += [high, (whole - high.astype(np.float32)).astype(jnp.bfloat16)]
    return np.stack(parts)


def split(value):
    high = value.astype(BF16)
    return high, (value - high.astype(F32)).astype(BF16)


def dot(left, right):
    return jnp.dot(left, right, preferred_element_type=F32)


def dot_nt(left, right):
    return lax.dot_general(left, right, (((1,), (1,)), ((), ())), preferred_element_type=F32)


def left_mul(high, low, value):
    vh, vl = split(value)
    return dot(jnp.concatenate([high, high, low], 1), jnp.concatenate([vh, vl, vh], 0))


def right_mul(value, high, low):
    vh, vl = split(value)
    return dot(jnp.concatenate([vh, vl, vh], 1), jnp.concatenate([high, high, low], 0))


def iota(shape, dim):
    return lax.broadcasted_iota(jnp.int32, shape, dim)


def onehot(hit):
    return jnp.where(hit, 1.0, 0.0).astype(BF16)


def kernel(
    n, groups, tab_count,
    vel_hbm, start_ref, *refs,
):
    staged = refs[: 7 + tab_count]
    upd, prs = refs[7 + tab_count : 9 + tab_count]
    vel = refs[9 + tab_count]
    local_refs = refs[10 + tab_count : 17 + 2 * tab_count]
    tlevel, trow, tcol, thrust, green, shift, ramp_tab = local_refs[:7]
    tab_y, tab_x = local_refs[7], local_refs[-1]
    (
        w_side, uv_side, h_src, h_side, fr_src, fr_buf, p_above,
        spec, modes, back, planes, m_hi, m_lo, mt_hi, mt_lo, inv,
        in_sem, halo_send, halo_recv, fr_send, fr_recv, pa_send, pa_recv,
        x_send, x_recv, y_send, y_recv,
    ) = refs[17 + 2 * tab_count :]
    levels, ny, nx = vel.shape[1:]
    rows = ny // n
    nz = levels * n
    nb = nz * rows
    me = lax.axis_index("gz")
    group = lax.axis_index("group")
    up = lax.rem(me + 1, n)
    down = lax.rem(me + n - 1, n)
    top = levels - 1

    loads = [
        pltpu.make_async_copy(src, dst, in_sem.at[i])
        for i, (src, dst) in enumerate(zip((vel_hbm, *staged), (vel, *local_refs)))
    ]
    for load in loads:
        load.start()

    barrier = pltpu.get_barrier_semaphore()

    @pl.loop(1, n)
    def _(off):
        pl.semaphore_signal(
            barrier, inc=1, device_id={"gz": lax.rem(me + off, n)}, device_id_type=MESH
        )

    for off in range(1, groups):
        pl.semaphore_signal(
            barrier, inc=1, device_id={"group": lax.rem(group + off, groups)}, device_id_type=MESH
        )
    pl.semaphore_wait(barrier, n - 1 + groups - 1)

    def remote(src, dst, send, recv, where):
        return pltpu.make_async_remote_copy(
            src_ref=src, dst_ref=dst, send_sem=send, recv_sem=recv,
            device_id=where, device_id_type=MESH,
        )

    inner = 1 - lax.rem(me, 2)
    outer = 1 - inner

    def there(side):
        return jnp.where(side == 1, me < n - 1, me > 0)

    def toward(side):
        return jnp.where(side == 1, up, down)

    uv = pl.ds(0, 2)

    def halo(src, dst, kind, side):
        return remote(
            src, dst.at[1 - side], halo_send.at[kind, side], halo_recv.at[kind, 1 - side],
            {"gz": toward(side)},
        )

    def halo_copy(kind, side):
        if kind == 0:
            return halo(vel_hbm.at[2, side * top], w_side, kind, side)
        if kind == 1:
            return halo(h_src.at[side], h_side, kind, side)
        return halo(vel_hbm.at[uv, side * top], uv_side, kind, side)

    def send(kind, side):
        @pl.when(there(side))
        def _():
            halo_copy(kind, side).start()

    def receive(kind, side):
        @pl.when(there(side))
        def _():
            halo_copy(kind, 1 - side).wait_recv()

    send(0, inner)
    send(0, outer)

    for side in range(2):

        @pl.when(jnp.logical_not(there(side)))
        def _():
            w_side[side] = jnp.zeros((ny, nx), F32)
            h_side[side] = jnp.zeros((ny, nx), F32)
            uv_side[side] = jnp.zeros((2, ny, nx), F32)
            if side == 1:
                p_above[...] = jnp.zeros((ny, nx), F32)

    for load in loads:
        load.wait()

    start = start_ref[0]
    pick = iota((FRINGE, nx), 1) - start == iota((FRINGE, nx), 0)
    pick_b = onehot(pick)
    fringe_copies = [
        remote(fr_src, fr_buf, fr_send.at[g - 1], fr_recv, {"group": g}) for g in range(1, groups)
    ]

    @pl.when(group == 0)
    def _():
        fr_buf[...] = jnp.zeros_like(fr_buf)
        for c in range(2):
            for k in range(levels):
                vh, vl = split(vel[c, k])
                fr_src[c * levels + k] = dot_nt(pick_b, vh) + dot_nt(pick_b, vl)
        for copy in fringe_copies:
            copy.start()

    is_farm = jnp.where(group > 0, 1.0, 0.0)
    ramp = is_farm * jnp.sum(jnp.where(pick, ramp_tab[...], 0.0), axis=0, keepdims=True)
    keep = 1.0 - ramp

    r_y = (tab_y[0], tab_y[1])
    rt_y = (tab_y[2], tab_y[3])
    d_y = (tab_y[4], tab_y[5])
    r_x = (tab_x[0], tab_x[1])
    rt_x = (tab_x[2], tab_x[3])
    d_x = (tab_x[4], tab_x[5])

    def dx(value):
        return -right_mul(value, *d_x)

    def dy(value):
        return left_mul(*d_y, value)

    turbines = trow.shape[1]
    pick_row = iota((ny, turbines), 0) == trow[...]
    pick_col = onehot(iota((nx, turbines), 0) == tcol[...])

    def predict(c, k):
        field = vel[c, k]
        if k < top and k > 0:
            vertical = vel[c, k + 1] - vel[c, k - 1]
        elif k < top:
            vertical = vel[c, k + 1]
        elif k > 0:
            vertical = -vel[c, k - 1]
        else:
            vertical = jnp.zeros_like(field)
        tend = -(vel[0, k] * dx(field) + vel[1, k] * dy(field) + (0.5 * vel[2, k]) * vertical)
        upd[c, k] = field + TIME_STEP * tend

    for k in range(levels):
        predict(2, k)

    half = 0.5 * TIME_STEP

    for side in (inner, outer):
        signed = half * (2 * side - 1).astype(F32)
        edge = side * top
        receive(0, side)
        w_there = w_side[side]
        upd[2, edge] = upd[2, edge] - signed * (vel[2, edge] * w_there)
        weight = (signed * keep) * w_there
        h_src[side] = (
            dx(weight * vel[0, edge])
            + dy(weight * vel[1, edge])
            - side.astype(F32) * upd[2, top]
        )
        send(1, side)

    speed = jnp.zeros((1, turbines), F32)
    for k in range(levels):
        vh, vl = split(vel[0, k])
        at_col = dot(vh, pick_col) + dot(vl, pick_col)
        here = jnp.sum(jnp.where(pick_row, at_col, 0.0), axis=0, keepdims=True)
        speed = speed + jnp.where(tlevel[...] == me * levels + k, here, 0.0)
    drag = (-TIME_STEP * is_farm) * thrust[...] * jnp.abs(speed) * speed
    for k in range(levels):
        predict(0, k)
        placed = jnp.where(pick_row & (tlevel[...] == me * levels + k), drag, 0.0)
        ph, pw = split(placed)
        upd[0, k] = upd[0, k] + dot_nt(ph, pick_col) + dot_nt(pw, pick_col)
        predict(1, k)

    @pl.when(group > 0)
    def _():
        fringe_copies[0].wait_recv()

    for k in range(levels):
        for c in range(2):
            th, tl = split(fr_buf[c * levels + k].T)
            upstream = dot(th, pick_b) + dot(tl, pick_b)
            predicted = upd[c, k]
            upd[c, k] = predicted + ramp * (upstream - predicted)

    for k in range(levels):
        divergence = dx(upd[0, k]) + dy(upd[1, k]) + upd[2, k]
        if k > 0:
            divergence = divergence - upd[2, k - 1]
        prs[k] = divergence

    rbits = rows.bit_length() - 1
    ybits = ny.bit_length() - 1
    eig = iota((nb, nz), 0) >> rbits == iota((nb, nz), 1)
    pos = iota((nb, nz), 0)
    lev = ((pos & (ny - 1)) >> rbits) * levels + (pos >> ybits) == iota((nb, nz), 1)
    eig_b, lev_b = onehot(eig), onehot(lev)
    same = (iota((nb, nb), 0) & (rows - 1)) == (iota((nb, nb), 1) & (rows - 1))
    for part, to, to_t in zip(split(green[...]), (m_hi, m_lo), (mt_hi, mt_lo)):
        wide = dot(eig_b, part).astype(BF16)
        to[...] = jnp.where(same, dot_nt(wide, lev_b), 0.0).astype(BF16)
        wide_t = dot_nt(lev_b, part).astype(BF16)
        to_t[...] = jnp.where(same, dot_nt(wide_t, eig_b), 0.0).astype(BF16)
    shifts = jnp.sum(jnp.where(eig, shift[...], 0.0), axis=1, keepdims=True)

    def wave_square(ids, length):
        wave = jnp.where(ids <= length // 2, ids, ids - length // 2)
        wave = wave.astype(F32) * (2.0 * np.pi / length)
        return wave * wave

    ky = me * rows + (iota((nb, 1), 0) & (rows - 1))
    kx = iota((1, nx), 1)
    inv[...] = 1.0 / (shifts + (wave_square(ky, ny) + wave_square(kx, nx)))

    def exchange(src, dst, send, recv):
        pltpu.make_async_copy(src.at[me], dst.at[me], recv).start()

        @pl.loop(1, n)
        def _(off):
            peer = lax.rem(me + off, n)
            remote(src.at[peer], dst.at[me], send, recv, {"gz": peer}).start()

    def arrived(dst, recv):
        pltpu.make_async_copy(dst, dst, recv).wait()

    def sent(src, send):
        most = src.at[pl.ds(0, n - 1)]
        pltpu.make_async_copy(most, most, send).wait()

    def transform(k):
        put(spec.at[k], right_mul(left_mul(*r_y, prs[k]), *rt_x), n)
        exchange(spec.at[k], modes.at[k], x_send.at[k], x_recv.at[k])

    for side in (inner, outer):
        edge = side * top
        receive(1, side)
        prs[edge] = prs[edge] + h_side[side]
        transform(edge)
    for k in range(1, top):
        transform(k)
    send(2, 1)

    scaled = None
    for k in range(top, -1, -1):
        arrived(modes.at[k], x_recv.at[k])
        cols = pl.ds(k * ny, ny)
        term = left_mul(m_hi[:, cols], m_lo[:, cols], get(modes.at[k]))
        scaled = term if scaled is None else scaled + term
    scaled = scaled * inv[...]
    for k in range(levels):
        own = pl.ds(k * ny, ny)
        put(back.at[k], left_mul(mt_hi[own], mt_lo[own], scaled), n)
        exchange(back.at[k], planes.at[k], y_send.at[k], y_recv.at[k])
    send(2, 0)

    receive(2, 0)
    for c in range(2):
        upd[c, 0] = upd[c, 0] + (half * keep) * (vel[2, 0] * uv_side[0, c])

    p_down = remote(prs.at[0], p_above, pa_send, pa_recv, {"gz": down})

    for k in range(levels):
        arrived(planes.at[k], y_recv.at[k])
        pressure = right_mul(left_mul(*rt_y, get(planes.at[k])), *r_x)
        prs[k] = pressure
        if k == 0:
            @pl.when(there(0))
            def _():
                p_down.start()

        else:
            upd[2, k - 1] = upd[2, k - 1] - (pressure - prs[k - 1])
        if k == top:
            receive(2, 1)
            for c in range(2):
                upd[c, top] = upd[c, top] - (half * keep) * (vel[2, top] * uv_side[1, c])
        upd[0, k] = upd[0, k] - dx(pressure)
        upd[1, k] = upd[1, k] - dy(pressure)

    @pl.when(there(1))
    def _():
        p_down.wait_recv()

    upd[2, top] = upd[2, top] - (p_above[...] - prs[top])

    for side in range(2):

        @pl.when(there(side))
        def _():
            for kind in range(3):
                halo_copy(kind, side).wait_send()

    @pl.when(there(0))
    def _():
        p_down.wait_send()

    @pl.when(group == 0)
    def _():
        for copy in fringe_copies:
            copy.wait_send()

    for k in range(levels):
        sent(spec.at[k], x_send.at[k])
        sent(back.at[k], y_send.at[k])


def put(ref, value, n):
    rows = ref.shape[1]
    if rows % 8 == 0:
        ref[...] = value.reshape(ref.shape)
    else:
        for i in range(n):
            ref[i] = value[i * rows : (i + 1) * rows]


def get(ref):
    n, rows, nx = ref.shape
    if rows % 8 == 0:
        return ref[...].reshape(n * rows, nx)
    return jnp.concatenate([ref[i] for i in range(n)], 0)


def local(
    n, groups,
    velocity, fringe_start, turbine_level, turbine_row, turbine_col, thrust, green_basis,
    eigen_shift,
):
    _, _, levels, ny, nx = velocity.shape
    rows = ny // n
    nz = levels * n
    nb = nz * rows
    offset = (np.arange(FRINGE) + 0.5)[:, None]
    ramp_tab = (np.sin(np.pi * offset / FRINGE) ** 2).astype(np.float32)
    hbm = pl.BlockSpec(memory_space=pltpu.HBM)
    vmem = pl.BlockSpec(memory_space=pltpu.VMEM)
    smem = pl.BlockSpec(memory_space=pltpu.SMEM)
    plane = (n, rows, nx)
    dma = pltpu.SemaphoreType.DMA
    tabs = [tables(length) for length in ((ny,) if ny == nx else (ny, nx))]
    staged = [
        turbine_level[None], turbine_row[None], turbine_col[None], thrust[None],
        green_basis, eigen_shift[None], ramp_tab, *tabs,
    ]
    fields = velocity[0]
    updated, pressure = pl.pallas_call(
        functools.partial(kernel, n, groups, len(tabs)),
        out_shape=(
            jax.ShapeDtypeStruct((3, levels, ny, nx), F32),
            jax.ShapeDtypeStruct((levels, ny, nx), F32),
        ),
        in_specs=[hbm, smem] + [hbm] * len(staged),
        out_specs=(vmem, vmem),
        scratch_shapes=[pltpu.VMEM(x.shape, x.dtype) for x in (fields, *staged)]
        + [
            pltpu.VMEM((2, ny, nx), F32),
            pltpu.VMEM((2, 2, ny, nx), F32),
            pltpu.VMEM((2, ny, nx), F32),
            pltpu.VMEM((2, ny, nx), F32),
            pltpu.VMEM((2 * levels, FRINGE, ny), F32),
            pltpu.VMEM((2 * levels, FRINGE, ny), F32),
            pltpu.VMEM((ny, nx), F32),
            pltpu.VMEM((levels, *plane), F32),
            pltpu.VMEM((levels, *plane), F32),
            pltpu.VMEM((levels, *plane), F32),
            pltpu.VMEM((levels, *plane), F32),
            pltpu.VMEM((nb, nb), BF16),
            pltpu.VMEM((nb, nb), BF16),
            pltpu.VMEM((nb, nb), BF16),
            pltpu.VMEM((nb, nb), BF16),
            pltpu.VMEM((nb, nx), F32),
            dma((1 + len(staged),)),
            dma((3, 2)),
            dma((3, 2)),
            dma((max(groups - 1, 1),)),
            dma,
            dma,
            dma,
            dma((levels,)),
            dma((levels,)),
            dma((levels,)),
            dma((levels,)),
        ],
        compiler_params=pltpu.CompilerParams(
            collective_id=0, has_side_effects=True, vmem_limit_bytes=40 * 1024 * 1024
        ),
        name="fractional_step",
    )(fields, fringe_start, *staged)
    return updated[None], pressure[None]


def solution(mesh):
    return jax.shard_map(
        functools.partial(local, mesh.shape["gz"], mesh.shape["group"]),
        mesh=mesh,
        in_specs=(P("group", None, "gz", None, None), P(), P(), P(), P(), P(), P(), P()),
        out_specs=(P("group", None, "gz", None, None), P("group", "gz", None, None)),
        check_vma=False,
    )
```

```python
import functools

import jax
import jax.numpy as jnp
import numpy as np
from jax import lax
from jax.experimental import pallas as pl
from jax.experimental.pallas import tpu as pltpu
from jax.sharding import PartitionSpec as P

FRINGE = 32
TIME_STEP = 0.25
MESH = pl.DeviceIdType.MESH
F32 = jnp.float32
BF16 = jnp.bfloat16


def tables(length):
    ids = np.arange(length)
    middle = length // 2
    wave = np.where(ids <= middle, ids, ids - middle)
    phases = 2.0 * np.pi / length * ((wave[:, None] * ids[None, :]) % length)
    norm = np.sqrt(np.where((ids == 0) | (ids == middle), 1.0, 2.0) / length)[:, None]
    basis = np.where(ids[:, None] <= middle, np.cos(phases), np.sin(phases)) * norm
    coupling = np.zeros((length, length))
    inner = np.arange(1, middle)
    coupling[inner, inner + middle] = 2.0 * np.pi * inner / length
    coupling[inner + middle, inner] = -2.0 * np.pi * inner / length
    deriv = basis.T @ coupling @ basis
    deriv = 0.5 * (deriv - deriv.T)
    parts = []
    for matrix in (basis, basis.T, deriv):
        whole = matrix.astype(np.float32)
        high = whole.astype(jnp.bfloat16)
        parts += [high, (whole - high.astype(np.float32)).astype(jnp.bfloat16)]
    return np.stack(parts)


def split(value):
    high = value.astype(BF16)
    return high, (value - high.astype(F32)).astype(BF16)


def dot(left, right):
    return jnp.dot(left, right, preferred_element_type=F32)


def dot_nt(left, right):
    return lax.dot_general(left, right, (((1,), (1,)), ((), ())), preferred_element_type=F32)


def left_mul(high, low, value):
    vh, vl = split(value)
    return dot(jnp.concatenate([high, high, low], 1), jnp.concatenate([vh, vl, vh], 0))


def right_mul(value, high, low):
    vh, vl = split(value)
    return dot(jnp.concatenate([vh, vl, vh], 1), jnp.concatenate([high, high, low], 0))


def iota(shape, dim):
    return lax.broadcasted_iota(jnp.int32, shape, dim)


def onehot(hit):
    return jnp.where(hit, 1.0, 0.0).astype(BF16)


def kernel(
    n, groups, tab_count,
    vel_hbm, start_ref, *refs,
):
    staged = refs[: 7 + tab_count]
    upd_hbm, prs_hbm = refs[7 + tab_count : 9 + tab_count]
    vel = refs[9 + tab_count]
    local_refs = refs[10 + tab_count : 17 + 2 * tab_count]
    tlevel, trow, tcol, thrust, green, shift, ramp_tab = local_refs[:7]
    tab_y, tab_x = local_refs[7], local_refs[-1]
    (
        upd, prs, zeros, w_side, uv_side, h_src, h_side, fr_src, fr_buf,
        spec, modes, back, planes, m_hi, m_lo, mt_hi, mt_lo, inv,
        in_sem, out_sem, halo_send, halo_recv, fr_send, fr_recv, pa_send, pa_recv,
        x_send, x_recv, y_send, y_recv,
    ) = refs[17 + 2 * tab_count :]
    levels, ny, nx = vel.shape[1:]
    rows = ny // n
    nz = levels * n
    nb = nz * rows
    me = lax.axis_index("gz")
    group = lax.axis_index("group")
    up = lax.rem(me + 1, n)
    down = lax.rem(me + n - 1, n)
    top = levels - 1

    loads = [
        pltpu.make_async_copy(src, dst, in_sem.at[i])
        for i, (src, dst) in enumerate(zip((vel_hbm, *staged), (vel, *local_refs)))
    ]
    for load in loads:
        load.start()

    barrier = pltpu.get_barrier_semaphore()

    @pl.loop(1, n)
    def _(off):
        pl.semaphore_signal(
            barrier, inc=1, device_id={"gz": lax.rem(me + off, n)}, device_id_type=MESH
        )

    for off in range(1, groups):
        pl.semaphore_signal(
            barrier, inc=1, device_id={"group": lax.rem(group + off, groups)}, device_id_type=MESH
        )
    pl.semaphore_wait(barrier, n - 1 + groups - 1)

    def remote(src, dst, send, recv, where):
        return pltpu.make_async_remote_copy(
            src_ref=src, dst_ref=dst, send_sem=send, recv_sem=recv,
            device_id=where, device_id_type=MESH,
        )

    inner = 1 - lax.rem(me, 2)
    outer = 1 - inner

    def there(side):
        return jnp.where(side == 1, me < n - 1, me > 0)

    def toward(side):
        return jnp.where(side == 1, up, down)

    uv = pl.ds(0, 2)

    def halo(src, dst, kind, side):
        return remote(
            src, dst.at[1 - side], halo_send.at[kind, side], halo_recv.at[kind, 1 - side],
            {"gz": toward(side)},
        )

    def halo_copy(kind, side):
        if kind == 0:
            return halo(vel_hbm.at[2, side * top], w_side, kind, side)
        if kind == 1:
            return halo(h_src.at[side], h_side, kind, side)
        return halo(vel_hbm.at[uv, side * top], uv_side, kind, side)

    def send(kind, side):
        @pl.when(there(side))
        def _():
            halo_copy(kind, side).start()

    def receive(kind, side):
        @pl.when(there(side))
        def _():
            halo_copy(kind, 1 - side).wait_recv()

    send(0, inner)
    send(0, outer)

    for side in range(2):

        @pl.when(jnp.logical_not(there(side)))
        def _():
            w_side[side] = jnp.zeros((ny, nx), F32)
            h_side[side] = jnp.zeros((ny, nx), F32)
            uv_side[side] = jnp.zeros((2, ny, nx), F32)

    for load in loads:
        load.wait()

    start = start_ref[0]
    pick = iota((FRINGE, nx), 1) - start == iota((FRINGE, nx), 0)
    pick_b = onehot(pick)
    fringe_copies = [
        remote(fr_src, fr_buf, fr_send.at[g - 1], fr_recv, {"group": g}) for g in range(1, groups)
    ]

    @pl.when(group == 0)
    def _():
        fr_buf[...] = jnp.zeros_like(fr_buf)
        for c in range(2):
            for k in range(levels):
                vh, vl = split(vel[c, k])
                fr_src[c * levels + k] = dot_nt(pick_b, vh) + dot_nt(pick_b, vl)
        for copy in fringe_copies:
            copy.start()

    is_farm = jnp.where(group > 0, 1.0, 0.0)
    ramp = is_farm * jnp.sum(jnp.where(pick, ramp_tab[...], 0.0), axis=0, keepdims=True)
    keep = 1.0 - ramp

    r_y = (tab_y[0], tab_y[1])
    rt_y = (tab_y[2], tab_y[3])
    d_y = (tab_y[4], tab_y[5])
    r_x = (tab_x[0], tab_x[1])
    rt_x = (tab_x[2], tab_x[3])
    d_x = (tab_x[4], tab_x[5])

    def dx(value):
        return -right_mul(value, *d_x)

    def dy(value):
        return left_mul(*d_y, value)

    turbines = trow.shape[1]
    pick_row = iota((ny, turbines), 0) == trow[...]
    pick_col = onehot(iota((nx, turbines), 0) == tcol[...])

    def predict(c, k):
        field = vel[c, k]
        if k < top and k > 0:
            vertical = vel[c, k + 1] - vel[c, k - 1]
        elif k < top:
            vertical = vel[c, k + 1]
        elif k > 0:
            vertical = -vel[c, k - 1]
        else:
            vertical = jnp.zeros_like(field)
        tend = -(vel[0, k] * dx(field) + vel[1, k] * dy(field) + (0.5 * vel[2, k]) * vertical)
        upd[c, k] = field + TIME_STEP * tend

    for k in range(levels):
        predict(2, k)

    half = 0.5 * TIME_STEP

    for side in (inner, outer):
        signed = half * (2 * side - 1).astype(F32)
        edge = side * top
        receive(0, side)
        w_there = w_side[side]
        upd[2, edge] = upd[2, edge] - signed * (vel[2, edge] * w_there)
        weight = (signed * keep) * w_there
        h_src[side] = (
            dx(weight * vel[0, edge])
            + dy(weight * vel[1, edge])
            - side.astype(F32) * upd[2, top]
        )
        send(1, side)

    speed = jnp.zeros((1, turbines), F32)
    for k in range(levels):
        vh, vl = split(vel[0, k])
        at_col = dot(vh, pick_col) + dot(vl, pick_col)
        here = jnp.sum(jnp.where(pick_row, at_col, 0.0), axis=0, keepdims=True)
        speed = speed + jnp.where(tlevel[...] == me * levels + k, here, 0.0)
    drag = (-TIME_STEP * is_farm) * thrust[...] * jnp.abs(speed) * speed
    for k in range(levels):
        predict(0, k)
        placed = jnp.where(pick_row & (tlevel[...] == me * levels + k), drag, 0.0)
        ph, pw = split(placed)
        upd[0, k] = upd[0, k] + dot_nt(ph, pick_col) + dot_nt(pw, pick_col)
        predict(1, k)

    @pl.when(group > 0)
    def _():
        fringe_copies[0].wait_recv()

    for k in range(levels):
        for c in range(2):
            th, tl = split(fr_buf[c * levels + k].T)
            upstream = dot(th, pick_b) + dot(tl, pick_b)
            predicted = upd[c, k]
            upd[c, k] = predicted + ramp * (upstream - predicted)

    for k in range(levels):
        divergence = dx(upd[0, k]) + dy(upd[1, k]) + upd[2, k]
        if k > 0:
            divergence = divergence - upd[2, k - 1]
        prs[k] = divergence

    rbits = rows.bit_length() - 1
    ybits = ny.bit_length() - 1
    eig = iota((nb, nz), 0) >> rbits == iota((nb, nz), 1)
    pos = iota((nb, nz), 0)
    lev = ((pos & (ny - 1)) >> rbits) * levels + (pos >> ybits) == iota((nb, nz), 1)
    eig_b, lev_b = onehot(eig), onehot(lev)
    same = (iota((nb, nb), 0) & (rows - 1)) == (iota((nb, nb), 1) & (rows - 1))
    for part, to, to_t in zip(split(green[...]), (m_hi, m_lo), (mt_hi, mt_lo)):
        wide = dot(eig_b, part).astype(BF16)
        to[...] = jnp.where(same, dot_nt(wide, lev_b), 0.0).astype(BF16)
        wide_t = dot_nt(lev_b, part).astype(BF16)
        to_t[...] = jnp.where(same, dot_nt(wide_t, eig_b), 0.0).astype(BF16)
    shifts = jnp.sum(jnp.where(eig, shift[...], 0.0), axis=1, keepdims=True)

    def wave_square(ids, length):
        wave = jnp.where(ids <= length // 2, ids, ids - length // 2)
        wave = wave.astype(F32) * (2.0 * np.pi / length)
        return wave * wave

    ky = me * rows + (iota((nb, 1), 0) & (rows - 1))
    kx = iota((1, nx), 1)
    inv[...] = 1.0 / (shifts + (wave_square(ky, ny) + wave_square(kx, nx)))

    def exchange(src, dst, send, recv):
        pltpu.make_async_copy(src.at[me], dst.at[me], recv).start()

        @pl.loop(1, n)
        def _(off):
            peer = lax.rem(me + off, n)
            remote(src.at[peer], dst.at[me], send, recv, {"gz": peer}).start()

    def arrived(dst, recv):
        pltpu.make_async_copy(dst, dst, recv).wait()

    def sent(src, send):
        most = src.at[pl.ds(0, n - 1)]
        pltpu.make_async_copy(most, most, send).wait()

    def transform(k):
        put(spec.at[k], right_mul(left_mul(*r_y, prs[k]), *rt_x), n)
        exchange(spec.at[k], modes.at[k], x_send.at[k], x_recv.at[k])

    for side in (inner, outer):
        edge = side * top
        receive(1, side)
        if side is outer:
            send(2, 0)
            send(2, 1)
        prs[edge] = prs[edge] + h_side[side]
        transform(edge)
    for k in range(1, top):
        transform(k)

    scaled = None
    for k in range(top, -1, -1):
        arrived(modes.at[k], x_recv.at[k])
        cols = pl.ds(k * ny, ny)
        term = left_mul(m_hi[:, cols], m_lo[:, cols], get(modes.at[k]))
        scaled = term if scaled is None else scaled + term
    scaled = scaled * inv[...]
    for k in range(levels):
        own = pl.ds(k * ny, ny)
        put(back.at[k], left_mul(mt_hi[own], mt_lo[own], scaled), n)
        exchange(back.at[k], planes.at[k], y_send.at[k], y_recv.at[k])
    for side in range(2):
        edge = side * top
        signed = half * (2 * side - 1)
        receive(2, side)
        for c in range(2):
            upd[c, edge] = upd[c, edge] - (signed * keep) * (vel[2, edge] * uv_side[side, c])
    out_upd = pltpu.make_async_copy(upd, upd_hbm, out_sem.at[0])
    out_upd.start()

    p_down = remote(prs.at[0], prs_hbm.at[levels], pa_send, pa_recv, {"gz": down})
    no_above = pltpu.make_async_copy(zeros, prs_hbm.at[levels], out_sem.at[1])

    @pl.when(jnp.logical_not(there(1)))
    def _():
        zeros[...] = jnp.zeros((ny, nx), F32)
        no_above.start()

    out_prs = []
    for k in range(levels):
        arrived(planes.at[k], y_recv.at[k])
        prs[k] = right_mul(left_mul(*rt_y, get(planes.at[k])), *r_x)
        if k == 0:

            @pl.when(there(0))
            def _():
                p_down.start()

        copy = pltpu.make_async_copy(prs.at[k], prs_hbm.at[k], out_sem.at[2 + k])
        copy.start()
        out_prs.append(copy)

    @pl.when(there(1))
    def _():
        p_down.wait_recv()

    @pl.when(jnp.logical_not(there(1)))
    def _():
        no_above.wait()

    out_upd.wait()
    for copy in out_prs:
        copy.wait()

    for side in range(2):

        @pl.when(there(side))
        def _():
            for kind in range(3):
                halo_copy(kind, side).wait_send()

    @pl.when(there(0))
    def _():
        p_down.wait_send()

    @pl.when(group == 0)
    def _():
        for copy in fringe_copies:
            copy.wait_send()

    for k in range(levels):
        sent(spec.at[k], x_send.at[k])
        sent(back.at[k], y_send.at[k])


def correct(base_hbm, planes_hbm, dy_hbm, dx_hbm, upd_hbm, prs_hbm, upd, prs, d_y, d_x, sem, out_sem):
    levels = prs_hbm.shape[0]
    loads = [
        pltpu.make_async_copy(src, dst, sem.at[i])
        for i, (src, dst) in enumerate(
            [(planes_hbm.at[k], prs.at[k]) for k in range(levels)]
            + [
                (dx_hbm, d_x),
                (dy_hbm, d_y),
                (base_hbm.at[pl.ds(0, 2)], upd.at[pl.ds(0, 2)]),
                (planes_hbm.at[levels], prs.at[levels]),
                (base_hbm.at[2], upd.at[2]),
            ]
        )
    ]
    for load in loads:
        load.start()
    whole = pltpu.make_async_copy(planes_hbm.at[pl.ds(0, levels)], prs_hbm, out_sem.at[levels])
    whole.start()
    for load in loads[: levels + 3]:
        load.wait()
    outs = []
    uv = pl.ds(0, 2)
    for k in range(levels):
        pressure = prs[k]
        upd[0, k] = upd[0, k] + right_mul(pressure, d_x[0], d_x[1])
        upd[1, k] = upd[1, k] - left_mul(d_y[0], d_y[1], pressure)
        outs.append(pltpu.make_async_copy(upd.at[uv, k], upd_hbm.at[uv, k], out_sem.at[k]))
        outs[-1].start()
    for load in loads[levels + 3 :]:
        load.wait()
    for k in range(levels):
        upd[2, k] = upd[2, k] - (prs[k + 1] - prs[k])
    last = pltpu.make_async_copy(upd.at[2], upd_hbm.at[2], sem.at[levels + 5])
    last.start()
    for copy in (whole, *outs, last):
        copy.wait()


def put(ref, value, n):
    rows = ref.shape[1]
    if rows % 8 == 0:
        ref[...] = value.reshape(ref.shape)
    else:
        for i in range(n):
            ref[i] = value[i * rows : (i + 1) * rows]


def get(ref):
    n, rows, nx = ref.shape
    if rows % 8 == 0:
        return ref[...].reshape(n * rows, nx)
    return jnp.concatenate([ref[i] for i in range(n)], 0)


def local(
    n, groups,
    velocity, fringe_start, turbine_level, turbine_row, turbine_col, thrust, green_basis,
    eigen_shift,
):
    _, _, levels, ny, nx = velocity.shape
    rows = ny // n
    nz = levels * n
    nb = nz * rows
    offset = (np.arange(FRINGE) + 0.5)[:, None]
    ramp_tab = (np.sin(np.pi * offset / FRINGE) ** 2).astype(np.float32)
    hbm = pl.BlockSpec(memory_space=pltpu.HBM)
    smem = pl.BlockSpec(memory_space=pltpu.SMEM)
    plane = (n, rows, nx)
    dma = pltpu.SemaphoreType.DMA
    tabs = [tables(length) for length in ((ny,) if ny == nx else (ny, nx))]
    staged = [
        turbine_level[None], turbine_row[None], turbine_col[None], thrust[None],
        green_basis, eigen_shift[None], ramp_tab, *tabs,
    ]
    fields = velocity[0]
    base, planes = pl.pallas_call(
        functools.partial(kernel, n, groups, len(tabs)),
        out_shape=(
            jax.ShapeDtypeStruct((3, levels, ny, nx), F32),
            jax.ShapeDtypeStruct((levels + 1, ny, nx), F32),
        ),
        in_specs=[hbm, smem] + [hbm] * len(staged),
        out_specs=(hbm, hbm),
        scratch_shapes=[pltpu.VMEM(x.shape, x.dtype) for x in (fields, *staged)]
        + [
            pltpu.VMEM((3, levels, ny, nx), F32),
            pltpu.VMEM((levels, ny, nx), F32),
            pltpu.VMEM((ny, nx), F32),
            pltpu.VMEM((2, ny, nx), F32),
            pltpu.VMEM((2, 2, ny, nx), F32),
            pltpu.VMEM((2, ny, nx), F32),
            pltpu.VMEM((2, ny, nx), F32),
            pltpu.VMEM((2 * levels, FRINGE, ny), F32),
            pltpu.VMEM((2 * levels, FRINGE, ny), F32),
            pltpu.VMEM((levels, *plane), F32),
            pltpu.VMEM((levels, *plane), F32),
            pltpu.VMEM((levels, *plane), F32),
            pltpu.VMEM((levels, *plane), F32),
            pltpu.VMEM((nb, nb), BF16),
            pltpu.VMEM((nb, nb), BF16),
            pltpu.VMEM((nb, nb), BF16),
            pltpu.VMEM((nb, nb), BF16),
            pltpu.VMEM((nb, nx), F32),
            dma((1 + len(staged),)),
            dma((2 + levels,)),
            dma((3, 2)),
            dma((3, 2)),
            dma((max(groups - 1, 1),)),
            dma,
            dma,
            dma,
            dma((levels,)),
            dma((levels,)),
            dma((levels,)),
            dma((levels,)),
        ],
        compiler_params=pltpu.CompilerParams(
            collective_id=0, has_side_effects=True, vmem_limit_bytes=58 * 1024 * 1024
        ),
        name="fractional_step",
    )(fields, fringe_start, *staged)
    derivs = [tab[4:] for tab in tabs]
    updated, pressure = pl.pallas_call(
        correct,
        out_shape=(
            jax.ShapeDtypeStruct((3, levels, ny, nx), F32),
            jax.ShapeDtypeStruct((levels, ny, nx), F32),
        ),
        in_specs=[hbm] * 4,
        out_specs=(hbm, hbm),
        scratch_shapes=[
            pltpu.VMEM((3, levels, ny, nx), F32),
            pltpu.VMEM((levels + 1, ny, nx), F32),
            pltpu.VMEM((2, ny, ny), BF16),
            pltpu.VMEM((2, nx, nx), BF16),
            dma((levels + 6,)),
            dma((levels + 1,)),
        ],
        compiler_params=pltpu.CompilerParams(vmem_limit_bytes=58 * 1024 * 1024),
        name="correction",
    )(base, planes, derivs[0], derivs[-1])
    return updated[None], pressure[None]


def solution(mesh):
    return jax.shard_map(
        functools.partial(local, mesh.shape["gz"], mesh.shape["group"]),
        mesh=mesh,
        in_specs=(P("group", None, "gz", None, None), P(), P(), P(), P(), P(), P(), P()),
        out_specs=(P("group", None, "gz", None, None), P("group", "gz", None, None)),
        check_vma=False,
    )
```

```python
import functools

import jax
import jax.numpy as jnp
import numpy as np
from jax import lax
from jax.experimental import pallas as pl
from jax.experimental.pallas import tpu as pltpu
from jax.sharding import PartitionSpec as P

FRINGE = 32
TIME_STEP = 0.25
MESH = pl.DeviceIdType.MESH
F32 = jnp.float32
BF16 = jnp.bfloat16


def tables(length):
    ids = np.arange(length)
    middle = length // 2
    wave = np.where(ids <= middle, ids, ids - middle)
    phases = 2.0 * np.pi / length * ((wave[:, None] * ids[None, :]) % length)
    norm = np.sqrt(np.where((ids == 0) | (ids == middle), 1.0, 2.0) / length)[:, None]
    basis = np.where(ids[:, None] <= middle, np.cos(phases), np.sin(phases)) * norm
    coupling = np.zeros((length, length))
    inner = np.arange(1, middle)
    coupling[inner, inner + middle] = 2.0 * np.pi * inner / length
    coupling[inner + middle, inner] = -2.0 * np.pi * inner / length
    deriv = basis.T @ coupling @ basis
    deriv = 0.5 * (deriv - deriv.T)
    parts = []
    for matrix in (basis, basis.T, deriv):
        whole = matrix.astype(np.float32)
        high = whole.astype(jnp.bfloat16)
        parts += [high, (whole - high.astype(np.float32)).astype(jnp.bfloat16)]
    return np.stack(parts)


def split(value):
    high = value.astype(BF16)
    return high, (value - high.astype(F32)).astype(BF16)


def dot(left, right):
    return jnp.dot(left, right, preferred_element_type=F32)


def dot_nt(left, right):
    return lax.dot_general(left, right, (((1,), (1,)), ((), ())), preferred_element_type=F32)


def left_mul(high, low, value):
    vh, vl = split(value)
    return dot(jnp.concatenate([high, high, low], 1), jnp.concatenate([vh, vl, vh], 0))


def right_mul(value, high, low):
    vh, vl = split(value)
    return dot(jnp.concatenate([vh, vl, vh], 1), jnp.concatenate([high, high, low], 0))


def iota(shape, dim):
    return lax.broadcasted_iota(jnp.int32, shape, dim)


def onehot(hit):
    return jnp.where(hit, 1.0, 0.0).astype(BF16)


def kernel(
    n, groups, tab_count,
    vel_hbm, start_ref, *refs,
):
    staged = refs[: 7 + tab_count]
    upd_hbm, prs_hbm = refs[7 + tab_count : 9 + tab_count]
    vel = refs[9 + tab_count]
    local_refs = refs[10 + tab_count : 17 + 2 * tab_count]
    tlevel, trow, tcol, thrust, green, shift, ramp_tab = local_refs[:7]
    tab_y, tab_x = local_refs[7], local_refs[-1]
    (
        upd, prs, p_above, w_side, uv_side, h_src, h_side, fr_src, fr_buf,
        spec, modes, back, planes, m_hi, m_lo, mt_hi, mt_lo, inv,
        in_sem, out_sem, halo_send, halo_recv, fr_send, fr_recv, pa_send, pa_recv,
        x_send, x_recv, y_send, y_recv,
    ) = refs[17 + 2 * tab_count :]
    levels, ny, nx = vel.shape[1:]
    rows = ny // n
    nz = levels * n
    nb = nz * rows
    me = lax.axis_index("gz")
    group = lax.axis_index("group")
    up = lax.rem(me + 1, n)
    down = lax.rem(me + n - 1, n)
    top = levels - 1

    loads = [
        pltpu.make_async_copy(src, dst, in_sem.at[i])
        for i, (src, dst) in enumerate(zip((vel_hbm, *staged), (vel, *local_refs)))
    ]
    for load in loads:
        load.start()

    barrier = pltpu.get_barrier_semaphore()

    @pl.loop(1, n)
    def _(off):
        pl.semaphore_signal(
            barrier, inc=1, device_id={"gz": lax.rem(me + off, n)}, device_id_type=MESH
        )

    for off in range(1, groups):
        pl.semaphore_signal(
            barrier, inc=1, device_id={"group": lax.rem(group + off, groups)}, device_id_type=MESH
        )
    loads[0].wait()
    pl.semaphore_wait(barrier, n - 1 + groups - 1)

    def remote(src, dst, send, recv, where):
        return pltpu.make_async_remote_copy(
            src_ref=src, dst_ref=dst, send_sem=send, recv_sem=recv,
            device_id=where, device_id_type=MESH,
        )

    inner = 1 - lax.rem(me, 2)
    outer = 1 - inner

    def there(side):
        return jnp.where(side == 1, me < n - 1, me > 0)

    def toward(side):
        return jnp.where(side == 1, up, down)

    uv = pl.ds(0, 2)

    def halo(src, dst, kind, side):
        return remote(
            src, dst.at[1 - side], halo_send.at[kind, side], halo_recv.at[kind, 1 - side],
            {"gz": toward(side)},
        )

    def halo_copy(kind, side):
        if kind == 0:
            return halo(vel.at[2, side * top], w_side, kind, side)
        if kind == 1:
            return halo(h_src.at[side], h_side, kind, side)
        return halo(vel.at[uv, side * top], uv_side, kind, side)

    def send(kind, side):
        @pl.when(there(side))
        def _():
            halo_copy(kind, side).start()

    def receive(kind, side):
        @pl.when(there(side))
        def _():
            halo_copy(kind, 1 - side).wait_recv()

    send(0, inner)
    send(0, outer)

    for side in range(2):

        @pl.when(jnp.logical_not(there(side)))
        def _():
            w_side[side] = jnp.zeros((ny, nx), F32)
            h_side[side] = jnp.zeros((ny, nx), F32)
            uv_side[side] = jnp.zeros((2, ny, nx), F32)

    for load in loads[1:]:
        load.wait()

    start = start_ref[0]
    pick = iota((FRINGE, nx), 1) - start == iota((FRINGE, nx), 0)
    pick_b = onehot(pick)
    fringe_copies = [
        remote(fr_src, fr_buf, fr_send.at[g - 1], fr_recv, {"group": g}) for g in range(1, groups)
    ]

    @pl.when(group == 0)
    def _():
        fr_buf[...] = jnp.zeros_like(fr_buf)
        for c in range(2):
            for k in range(levels):
                vh, vl = split(vel[c, k])
                fr_src[c * levels + k] = dot_nt(pick_b, vh) + dot_nt(pick_b, vl)
        for copy in fringe_copies:
            copy.start()

    is_farm = jnp.where(group > 0, 1.0, 0.0)
    ramp = is_farm * jnp.sum(jnp.where(pick, ramp_tab[...], 0.0), axis=0, keepdims=True)
    keep = 1.0 - ramp

    r_y = (tab_y[0], tab_y[1])
    rt_y = (tab_y[2], tab_y[3])
    d_y = (tab_y[4], tab_y[5])
    r_x = (tab_x[0], tab_x[1])
    rt_x = (tab_x[2], tab_x[3])
    d_x = (tab_x[4], tab_x[5])

    def dx(value):
        return -right_mul(value, *d_x)

    def dy(value):
        return left_mul(*d_y, value)

    turbines = trow.shape[1]
    pick_row = iota((ny, turbines), 0) == trow[...]
    pick_col = onehot(iota((nx, turbines), 0) == tcol[...])

    def predict(c, k):
        field = vel[c, k]
        if k < top and k > 0:
            vertical = vel[c, k + 1] - vel[c, k - 1]
        elif k < top:
            vertical = vel[c, k + 1]
        elif k > 0:
            vertical = -vel[c, k - 1]
        else:
            vertical = jnp.zeros_like(field)
        tend = -(vel[0, k] * dx(field) + vel[1, k] * dy(field) + (0.5 * vel[2, k]) * vertical)
        upd[c, k] = field + TIME_STEP * tend

    for k in range(levels):
        predict(2, k)

    half = 0.5 * TIME_STEP

    for side in (inner, outer):
        signed = half * (2 * side - 1).astype(F32)
        edge = side * top
        receive(0, side)
        w_there = w_side[side]
        upd[2, edge] = upd[2, edge] - signed * (vel[2, edge] * w_there)
        weight = (signed * keep) * w_there
        h_src[side] = (
            dx(weight * vel[0, edge])
            + dy(weight * vel[1, edge])
            - side.astype(F32) * upd[2, top]
        )
        send(1, side)

    speed = jnp.zeros((1, turbines), F32)
    for k in range(levels):
        vh, vl = split(vel[0, k])
        at_col = dot(vh, pick_col) + dot(vl, pick_col)
        here = jnp.sum(jnp.where(pick_row, at_col, 0.0), axis=0, keepdims=True)
        speed = speed + jnp.where(tlevel[...] == me * levels + k, here, 0.0)
    drag = (-TIME_STEP * is_farm) * thrust[...] * jnp.abs(speed) * speed
    for k in range(levels):
        predict(0, k)
        placed = jnp.where(pick_row & (tlevel[...] == me * levels + k), drag, 0.0)
        ph, pw = split(placed)
        upd[0, k] = upd[0, k] + dot_nt(ph, pick_col) + dot_nt(pw, pick_col)
        predict(1, k)

    @pl.when(group > 0)
    def _():
        fringe_copies[0].wait_recv()

    for k in range(levels):
        for c in range(2):
            th, tl = split(fr_buf[c * levels + k].T)
            upstream = dot(th, pick_b) + dot(tl, pick_b)
            predicted = upd[c, k]
            upd[c, k] = predicted + ramp * (upstream - predicted)

    for k in range(levels):
        divergence = dx(upd[0, k]) + dy(upd[1, k]) + upd[2, k]
        if k > 0:
            divergence = divergence - upd[2, k - 1]
        prs[k] = divergence

    rbits = rows.bit_length() - 1
    ybits = ny.bit_length() - 1
    eig = iota((nb, nz), 0) >> rbits == iota((nb, nz), 1)
    pos = iota((nb, nz), 0)
    lev = ((pos & (ny - 1)) >> rbits) * levels + (pos >> ybits) == iota((nb, nz), 1)
    eig_b, lev_b = onehot(eig), onehot(lev)
    same = (iota((nb, nb), 0) & (rows - 1)) == (iota((nb, nb), 1) & (rows - 1))
    for part, to, to_t in zip(split(green[...]), (m_hi, m_lo), (mt_hi, mt_lo)):
        wide = dot(eig_b, part).astype(BF16)
        to[...] = jnp.where(same, dot_nt(wide, lev_b), 0.0).astype(BF16)
        wide_t = dot_nt(lev_b, part).astype(BF16)
        to_t[...] = jnp.where(same, dot_nt(wide_t, eig_b), 0.0).astype(BF16)
    shifts = jnp.sum(jnp.where(eig, shift[...], 0.0), axis=1, keepdims=True)

    def wave_square(ids, length):
        wave = jnp.where(ids <= length // 2, ids, ids - length // 2)
        wave = wave.astype(F32) * (2.0 * np.pi / length)
        return wave * wave

    ky = me * rows + (iota((nb, 1), 0) & (rows - 1))
    kx = iota((1, nx), 1)
    inv[...] = 1.0 / (shifts + (wave_square(ky, ny) + wave_square(kx, nx)))

    def exchange(src, dst, send, recv):
        pltpu.make_async_copy(src.at[me], dst.at[me], recv).start()

        @pl.loop(1, n)
        def _(off):
            peer = lax.rem(me + off, n)
            remote(src.at[peer], dst.at[me], send, recv, {"gz": peer}).start()

    def arrived(dst, recv):
        pltpu.make_async_copy(dst, dst, recv).wait()

    def sent(src, send):
        most = src.at[pl.ds(0, n - 1)]
        pltpu.make_async_copy(most, most, send).wait()

    def transform(k):
        put(spec.at[k], right_mul(left_mul(*r_y, prs[k]), *rt_x), n)
        exchange(spec.at[k], modes.at[k], x_send.at[k], x_recv.at[k])

    for side in (inner, outer):
        edge = side * top
        receive(1, side)
        if side is outer:
            send(2, 0)
            send(2, 1)
        prs[edge] = prs[edge] + h_side[side]
        transform(edge)
    for k in range(1, top):
        transform(k)

    scaled = None
    for k in range(top, -1, -1):
        arrived(modes.at[k], x_recv.at[k])
        cols = pl.ds(k * ny, ny)
        term = left_mul(m_hi[:, cols], m_lo[:, cols], get(modes.at[k]))
        scaled = term if scaled is None else scaled + term
    scaled = scaled * inv[...]
    for k in range(levels):
        own = pl.ds(k * ny, ny)
        put(back.at[k], left_mul(mt_hi[own], mt_lo[own], scaled), n)
        exchange(back.at[k], planes.at[k], y_send.at[k], y_recv.at[k])
    for side in range(2):
        edge = side * top
        signed = half * (2 * side - 1)
        receive(2, side)
        for c in range(2):
            upd[c, edge] = upd[c, edge] - (signed * keep) * (vel[2, edge] * uv_side[side, c])
    out_upd = pltpu.make_async_copy(upd, upd_hbm, out_sem.at[0])
    out_upd.start()

    p_down = remote(prs.at[0], p_above, pa_send, pa_recv, {"gz": down})

    @pl.when(jnp.logical_not(there(1)))
    def _():
        p_above[...] = jnp.zeros((ny, nx), F32)

    out_prs = []
    for k in range(levels):
        arrived(planes.at[k], y_recv.at[k])
        prs[k] = right_mul(left_mul(*rt_y, get(planes.at[k])), *r_x)
        if k == 0:

            @pl.when(there(0))
            def _():
                p_down.start()

        copy = pltpu.make_async_copy(prs.at[k], prs_hbm.at[k], out_sem.at[2 + k])
        copy.start()
        out_prs.append(copy)

    @pl.when(there(1))
    def _():
        p_down.wait_recv()

    out_above = pltpu.make_async_copy(p_above, prs_hbm.at[levels], out_sem.at[1])
    out_above.start()
    out_upd.wait()
    for copy in out_prs:
        copy.wait()
    out_above.wait()

    for side in range(2):

        @pl.when(there(side))
        def _():
            for kind in range(3):
                halo_copy(kind, side).wait_send()

    @pl.when(there(0))
    def _():
        p_down.wait_send()

    @pl.when(group == 0)
    def _():
        for copy in fringe_copies:
            copy.wait_send()

    for k in range(levels):
        sent(spec.at[k], x_send.at[k])
        sent(back.at[k], y_send.at[k])


def correct(base_hbm, planes_hbm, dy_hbm, dx_hbm, upd_hbm, prs_hbm, upd, prs, d_y, d_x, sem, out_sem):
    levels = prs_hbm.shape[0]
    loads = [
        pltpu.make_async_copy(src, dst, sem.at[i])
        for i, (src, dst) in enumerate(
            [(planes_hbm.at[k], prs.at[k]) for k in range(levels)]
            + [
                (dx_hbm, d_x),
                (dy_hbm, d_y),
                (base_hbm.at[pl.ds(0, 2)], upd.at[pl.ds(0, 2)]),
                (planes_hbm.at[levels], prs.at[levels]),
                (base_hbm.at[2], upd.at[2]),
            ]
        )
    ]
    for load in loads:
        load.start()
    for load in loads[: levels + 3]:
        load.wait()
    whole = pltpu.make_async_copy(prs.at[pl.ds(0, levels)], prs_hbm, out_sem.at[levels])
    whole.start()
    outs = []
    uv = pl.ds(0, 2)
    for k in range(levels):
        pressure = prs[k]
        upd[0, k] = upd[0, k] + right_mul(pressure, d_x[0], d_x[1])
        upd[1, k] = upd[1, k] - left_mul(d_y[0], d_y[1], pressure)
        outs.append(pltpu.make_async_copy(upd.at[uv, k], upd_hbm.at[uv, k], out_sem.at[k]))
        outs[-1].start()
    for load in loads[levels + 3 :]:
        load.wait()
    for k in range(levels):
        upd[2, k] = upd[2, k] - (prs[k + 1] - prs[k])
    last = pltpu.make_async_copy(upd.at[2], upd_hbm.at[2], sem.at[levels + 5])
    last.start()
    for copy in (whole, *outs, last):
        copy.wait()


def put(ref, value, n):
    rows = ref.shape[1]
    if rows % 8 == 0:
        ref[...] = value.reshape(ref.shape)
    else:
        for i in range(n):
            ref[i] = value[i * rows : (i + 1) * rows]


def get(ref):
    n, rows, nx = ref.shape
    if rows % 8 == 0:
        return ref[...].reshape(n * rows, nx)
    return jnp.concatenate([ref[i] for i in range(n)], 0)


def local(
    n, groups,
    velocity, fringe_start, turbine_level, turbine_row, turbine_col, thrust, green_basis,
    eigen_shift,
):
    _, _, levels, ny, nx = velocity.shape
    rows = ny // n
    nz = levels * n
    nb = nz * rows
    offset = (np.arange(FRINGE) + 0.5)[:, None]
    ramp_tab = (np.sin(np.pi * offset / FRINGE) ** 2).astype(np.float32)
    hbm = pl.BlockSpec(memory_space=pltpu.HBM)
    smem = pl.BlockSpec(memory_space=pltpu.SMEM)
    plane = (n, rows, nx)
    dma = pltpu.SemaphoreType.DMA
    tabs = [tables(length) for length in ((ny,) if ny == nx else (ny, nx))]
    staged = [
        turbine_level[None], turbine_row[None], turbine_col[None], thrust[None],
        green_basis, eigen_shift[None], ramp_tab, *tabs,
    ]
    fields = velocity[0]
    base, planes = pl.pallas_call(
        functools.partial(kernel, n, groups, len(tabs)),
        out_shape=(
            jax.ShapeDtypeStruct((3, levels, ny, nx), F32),
            jax.ShapeDtypeStruct((levels + 1, ny, nx), F32),
        ),
        in_specs=[hbm, smem] + [hbm] * len(staged),
        out_specs=(hbm, hbm),
        scratch_shapes=[pltpu.VMEM(x.shape, x.dtype) for x in (fields, *staged)]
        + [
            pltpu.VMEM((3, levels, ny, nx), F32),
            pltpu.VMEM((levels, ny, nx), F32),
            pltpu.VMEM((ny, nx), F32),
            pltpu.VMEM((2, ny, nx), F32),
            pltpu.VMEM((2, 2, ny, nx), F32),
            pltpu.VMEM((2, ny, nx), F32),
            pltpu.VMEM((2, ny, nx), F32),
            pltpu.VMEM((2 * levels, FRINGE, ny), F32),
            pltpu.VMEM((2 * levels, FRINGE, ny), F32),
            pltpu.VMEM((levels, *plane), F32),
            pltpu.VMEM((levels, *plane), F32),
            pltpu.VMEM((levels, *plane), F32),
            pltpu.VMEM((levels, *plane), F32),
            pltpu.VMEM((nb, nb), BF16),
            pltpu.VMEM((nb, nb), BF16),
            pltpu.VMEM((nb, nb), BF16),
            pltpu.VMEM((nb, nb), BF16),
            pltpu.VMEM((nb, nx), F32),
            dma((1 + len(staged),)),
            dma((2 + levels,)),
            dma((3, 2)),
            dma((3, 2)),
            dma((max(groups - 1, 1),)),
            dma,
            dma,
            dma,
            dma((levels,)),
            dma((levels,)),
            dma((levels,)),
            dma((levels,)),
        ],
        compiler_params=pltpu.CompilerParams(
            collective_id=0, has_side_effects=True, vmem_limit_bytes=58 * 1024 * 1024
        ),
        name="fractional_step",
    )(fields, fringe_start, *staged)
    derivs = [tab[4:] for tab in tabs]
    updated, pressure = pl.pallas_call(
        correct,
        out_shape=(
            jax.ShapeDtypeStruct((3, levels, ny, nx), F32),
            jax.ShapeDtypeStruct((levels, ny, nx), F32),
        ),
        in_specs=[hbm] * 4,
        out_specs=(hbm, hbm),
        scratch_shapes=[
            pltpu.VMEM((3, levels, ny, nx), F32),
            pltpu.VMEM((levels + 1, ny, nx), F32),
            pltpu.VMEM((2, ny, ny), BF16),
            pltpu.VMEM((2, nx, nx), BF16),
            dma((levels + 6,)),
            dma((levels + 1,)),
        ],
        compiler_params=pltpu.CompilerParams(vmem_limit_bytes=58 * 1024 * 1024),
        name="correction",
    )(base, planes, derivs[0], derivs[-1])
    return updated[None], pressure[None]


def solution(mesh):
    return jax.shard_map(
        functools.partial(local, mesh.shape["gz"], mesh.shape["group"]),
        mesh=mesh,
        in_specs=(P("group", None, "gz", None, None), P(), P(), P(), P(), P(), P(), P()),
        out_specs=(P("group", None, "gz", None, None), P("group", "gz", None, None)),
        check_vma=False,
    )
```

```python
import functools

import jax
import jax.numpy as jnp
import numpy as np
from jax import lax
from jax.experimental import pallas as pl
from jax.experimental.pallas import tpu as pltpu
from jax.sharding import PartitionSpec as P

FRINGE = 32
TIME_STEP = 0.25
MESH = pl.DeviceIdType.MESH
F32 = jnp.float32
BF16 = jnp.bfloat16


def tables(length):
    ids = np.arange(length)
    middle = length // 2
    wave = np.where(ids <= middle, ids, ids - middle)
    phases = 2.0 * np.pi / length * ((wave[:, None] * ids[None, :]) % length)
    norm = np.sqrt(np.where((ids == 0) | (ids == middle), 1.0, 2.0) / length)[:, None]
    basis = np.where(ids[:, None] <= middle, np.cos(phases), np.sin(phases)) * norm
    coupling = np.zeros((length, length))
    inner = np.arange(1, middle)
    coupling[inner, inner + middle] = 2.0 * np.pi * inner / length
    coupling[inner + middle, inner] = -2.0 * np.pi * inner / length
    deriv = basis.T @ coupling @ basis
    deriv = 0.5 * (deriv - deriv.T)
    parts = []
    for matrix in (basis, basis.T, deriv):
        whole = matrix.astype(np.float32)
        high = whole.astype(jnp.bfloat16)
        parts += [high, (whole - high.astype(np.float32)).astype(jnp.bfloat16)]
    return np.stack(parts)


def split(value):
    high = value.astype(BF16)
    return high, (value - high.astype(F32)).astype(BF16)


def dot(left, right):
    return jnp.dot(left, right, preferred_element_type=F32)


def dot_nt(left, right):
    return lax.dot_general(left, right, (((1,), (1,)), ((), ())), preferred_element_type=F32)


def left_mul(high, low, value):
    vh, vl = split(value)
    return dot(jnp.concatenate([high, high, low], 1), jnp.concatenate([vh, vl, vh], 0))


def right_mul(value, high, low):
    vh, vl = split(value)
    return dot(jnp.concatenate([vh, vl, vh], 1), jnp.concatenate([high, high, low], 0))


def iota(shape, dim):
    return lax.broadcasted_iota(jnp.int32, shape, dim)


def onehot(hit):
    return jnp.where(hit, 1.0, 0.0).astype(BF16)


def kernel(
    n, groups, tab_count,
    vel_hbm, start_ref, *refs,
):
    staged = refs[: 7 + tab_count]
    upd_hbm, prs_hbm = refs[7 + tab_count : 9 + tab_count]
    vel = refs[9 + tab_count]
    local_refs = refs[10 + tab_count : 17 + 2 * tab_count]
    tlevel, trow, tcol, thrust, green, shift, ramp_tab = local_refs[:7]
    tab_y, tab_x = local_refs[7], local_refs[-1]
    (
        upd, prs, p_above, w_side, uv_side, h_src, h_side, fr_src, fr_buf,
        spec, modes, back, planes, m_hi, m_lo, mt_hi, mt_lo, inv,
        in_sem, out_sem, halo_send, halo_recv, fr_send, fr_recv, pa_send, pa_recv,
        x_send, x_recv, y_send, y_recv,
    ) = refs[17 + 2 * tab_count :]
    levels, ny, nx = vel.shape[1:]
    rows = ny // n
    nz = levels * n
    nb = nz * rows
    me = lax.axis_index("gz")
    group = lax.axis_index("group")
    up = lax.rem(me + 1, n)
    down = lax.rem(me + n - 1, n)
    top = levels - 1

    loads = [
        pltpu.make_async_copy(src, dst, in_sem.at[i])
        for i, (src, dst) in enumerate(zip((vel_hbm, *staged), (vel, *local_refs)))
    ]
    for load in loads:
        load.start()

    barrier = pltpu.get_barrier_semaphore()

    @pl.loop(1, n)
    def _(off):
        pl.semaphore_signal(
            barrier, inc=1, device_id={"gz": lax.rem(me + off, n)}, device_id_type=MESH
        )

    for off in range(1, groups):
        pl.semaphore_signal(
            barrier, inc=1, device_id={"group": lax.rem(group + off, groups)}, device_id_type=MESH
        )
    loads[0].wait()
    pl.semaphore_wait(barrier, n - 1 + groups - 1)

    def remote(src, dst, send, recv, where):
        return pltpu.make_async_remote_copy(
            src_ref=src, dst_ref=dst, send_sem=send, recv_sem=recv,
            device_id=where, device_id_type=MESH,
        )

    inner = 1 - lax.rem(me, 2)
    outer = 1 - inner

    def there(side):
        return jnp.where(side == 1, me < n - 1, me > 0)

    def toward(side):
        return jnp.where(side == 1, up, down)

    uv = pl.ds(0, 2)

    def halo(src, dst, kind, side):
        return remote(
            src, dst.at[1 - side], halo_send.at[kind, side], halo_recv.at[kind, 1 - side],
            {"gz": toward(side)},
        )

    def halo_copy(kind, side):
        if kind == 0:
            return halo(vel.at[2, side * top], w_side, kind, side)
        if kind == 1:
            return halo(h_src.at[side], h_side, kind, side)
        return halo(vel.at[uv, side * top], uv_side, kind, side)

    def send(kind, side):
        @pl.when(there(side))
        def _():
            halo_copy(kind, side).start()

    def receive(kind, side):
        @pl.when(there(side))
        def _():
            halo_copy(kind, 1 - side).wait_recv()

    send(0, inner)
    send(0, outer)

    for side in range(2):

        @pl.when(jnp.logical_not(there(side)))
        def _():
            w_side[side] = jnp.zeros((ny, nx), F32)
            h_side[side] = jnp.zeros((ny, nx), F32)
            uv_side[side] = jnp.zeros((2, ny, nx), F32)

    for load in loads[1:]:
        load.wait()

    start = start_ref[0]
    pick = iota((FRINGE, nx), 1) - start == iota((FRINGE, nx), 0)
    pick_b = onehot(pick)
    fringe_copies = [
        remote(fr_src, fr_buf, fr_send.at[g - 1], fr_recv, {"group": g}) for g in range(1, groups)
    ]

    @pl.when(group == 0)
    def _():
        fr_buf[...] = jnp.zeros_like(fr_buf)
        for c in range(2):
            for k in range(levels):
                vh, vl = split(vel[c, k])
                fr_src[c * levels + k] = dot_nt(pick_b, vh) + dot_nt(pick_b, vl)
        for copy in fringe_copies:
            copy.start()

    is_farm = jnp.where(group > 0, 1.0, 0.0)
    ramp = is_farm * jnp.sum(jnp.where(pick, ramp_tab[...], 0.0), axis=0, keepdims=True)
    keep = 1.0 - ramp

    r_y = (tab_y[0], tab_y[1])
    rt_y = (tab_y[2], tab_y[3])
    d_y = (tab_y[4], tab_y[5])
    r_x = (tab_x[0], tab_x[1])
    rt_x = (tab_x[2], tab_x[3])
    d_x = (tab_x[4], tab_x[5])

    def dx(value):
        return -right_mul(value, *d_x)

    def dy(value):
        return left_mul(*d_y, value)

    turbines = trow.shape[1]
    pick_row = iota((ny, turbines), 0) == trow[...]
    pick_col = onehot(iota((nx, turbines), 0) == tcol[...])

    def predict(c, k):
        field = vel[c, k]
        if k < top and k > 0:
            vertical = vel[c, k + 1] - vel[c, k - 1]
        elif k < top:
            vertical = vel[c, k + 1]
        elif k > 0:
            vertical = -vel[c, k - 1]
        else:
            vertical = jnp.zeros_like(field)
        tend = -(vel[0, k] * dx(field) + vel[1, k] * dy(field) + (0.5 * vel[2, k]) * vertical)
        upd[c, k] = field + TIME_STEP * tend

    for k in range(levels):
        predict(2, k)

    half = 0.5 * TIME_STEP

    for side in (inner, outer):
        signed = half * (2 * side - 1).astype(F32)
        edge = side * top
        receive(0, side)
        w_there = w_side[side]
        upd[2, edge] = upd[2, edge] - signed * (vel[2, edge] * w_there)
        weight = (signed * keep) * w_there
        h_src[side] = (
            dx(weight * vel[0, edge])
            + dy(weight * vel[1, edge])
            - side.astype(F32) * upd[2, top]
        )
        send(1, side)

    speed = jnp.zeros((1, turbines), F32)
    for k in range(levels):
        vh, vl = split(vel[0, k])
        at_col = dot(vh, pick_col) + dot(vl, pick_col)
        here = jnp.sum(jnp.where(pick_row, at_col, 0.0), axis=0, keepdims=True)
        speed = speed + jnp.where(tlevel[...] == me * levels + k, here, 0.0)
    drag = (-TIME_STEP * is_farm) * thrust[...] * jnp.abs(speed) * speed
    for k in range(levels):
        predict(0, k)
        placed = jnp.where(pick_row & (tlevel[...] == me * levels + k), drag, 0.0)
        ph, pw = split(placed)
        upd[0, k] = upd[0, k] + dot_nt(ph, pick_col) + dot_nt(pw, pick_col)
        predict(1, k)

    @pl.when(group > 0)
    def _():
        fringe_copies[0].wait_recv()

    for k in range(levels):
        for c in range(2):
            th, tl = split(fr_buf[c * levels + k].T)
            upstream = dot(th, pick_b) + dot(tl, pick_b)
            predicted = upd[c, k]
            upd[c, k] = predicted + ramp * (upstream - predicted)

    for k in range(levels):
        divergence = dx(upd[0, k]) + dy(upd[1, k]) + upd[2, k]
        if k > 0:
            divergence = divergence - upd[2, k - 1]
        prs[k] = divergence

    rbits = rows.bit_length() - 1
    ybits = ny.bit_length() - 1
    eig = iota((nb, nz), 0) >> rbits == iota((nb, nz), 1)
    pos = iota((nb, nz), 0)
    lev = ((pos & (ny - 1)) >> rbits) * levels + (pos >> ybits) == iota((nb, nz), 1)
    eig_b, lev_b = onehot(eig), onehot(lev)
    same = (iota((nb, nb), 0) & (rows - 1)) == (iota((nb, nb), 1) & (rows - 1))
    for part, to, to_t in zip(split(green[...]), (m_hi, m_lo), (mt_hi, mt_lo)):
        wide = dot(eig_b, part).astype(BF16)
        to[...] = jnp.where(same, dot_nt(wide, lev_b), 0.0).astype(BF16)
        wide_t = dot_nt(lev_b, part).astype(BF16)
        to_t[...] = jnp.where(same, dot_nt(wide_t, eig_b), 0.0).astype(BF16)
    shifts = jnp.sum(jnp.where(eig, shift[...], 0.0), axis=1, keepdims=True)

    def wave_square(ids, length):
        wave = jnp.where(ids <= length // 2, ids, ids - length // 2)
        wave = wave.astype(F32) * (2.0 * np.pi / length)
        return wave * wave

    ky = me * rows + (iota((nb, 1), 0) & (rows - 1))
    kx = iota((1, nx), 1)
    inv[...] = 1.0 / (shifts + (wave_square(ky, ny) + wave_square(kx, nx)))

    def exchange(src, dst, send, recv):
        pltpu.make_async_copy(src.at[me], dst.at[me], recv).start()

        @pl.loop(1, n)
        def _(off):
            peer = lax.rem(me + off, n)
            remote(src.at[peer], dst.at[me], send, recv, {"gz": peer}).start()

    def arrived(dst, recv):
        pltpu.make_async_copy(dst, dst, recv).wait()

    def sent(src, send):
        most = src.at[pl.ds(0, n - 1)]
        pltpu.make_async_copy(most, most, send).wait()

    def transform(k):
        put(spec.at[k], right_mul(left_mul(*r_y, prs[k]), *rt_x), n)
        exchange(spec.at[k], modes.at[k], x_send.at[k], x_recv.at[k])

    for side in (inner, outer):
        edge = side * top
        receive(1, side)
        prs[edge] = prs[edge] + h_side[side]
        transform(edge)
    for k in range(1, top):
        transform(k)
    send(2, 1)

    scaled = None
    for k in range(top, -1, -1):
        arrived(modes.at[k], x_recv.at[k])
        cols = pl.ds(k * ny, ny)
        term = left_mul(m_hi[:, cols], m_lo[:, cols], get(modes.at[k]))
        scaled = term if scaled is None else scaled + term
    send(2, 0)
    scaled = scaled * inv[...]
    for k in range(levels):
        own = pl.ds(k * ny, ny)
        put(back.at[k], left_mul(mt_hi[own], mt_lo[own], scaled), n)
        exchange(back.at[k], planes.at[k], y_send.at[k], y_recv.at[k])
    for side in range(2):
        edge = side * top
        signed = half * (2 * side - 1)
        receive(2, side)
        for c in range(2):
            upd[c, edge] = upd[c, edge] - (signed * keep) * (vel[2, edge] * uv_side[side, c])
    out_upd = pltpu.make_async_copy(upd, upd_hbm, out_sem.at[0])
    out_upd.start()

    p_down = remote(prs.at[0], p_above, pa_send, pa_recv, {"gz": down})

    @pl.when(jnp.logical_not(there(1)))
    def _():
        p_above[...] = jnp.zeros((ny, nx), F32)

    out_prs = []
    for k in range(levels):
        arrived(planes.at[k], y_recv.at[k])
        prs[k] = right_mul(left_mul(*rt_y, get(planes.at[k])), *r_x)
        if k == 0:

            @pl.when(there(0))
            def _():
                p_down.start()

        copy = pltpu.make_async_copy(prs.at[k], prs_hbm.at[k], out_sem.at[2 + k])
        copy.start()
        out_prs.append(copy)

    @pl.when(there(1))
    def _():
        p_down.wait_recv()

    out_above = pltpu.make_async_copy(p_above, prs_hbm.at[levels], out_sem.at[1])
    out_above.start()
    out_upd.wait()
    for copy in out_prs:
        copy.wait()
    out_above.wait()

    for side in range(2):

        @pl.when(there(side))
        def _():
            for kind in range(3):
                halo_copy(kind, side).wait_send()

    @pl.when(there(0))
    def _():
        p_down.wait_send()

    @pl.when(group == 0)
    def _():
        for copy in fringe_copies:
            copy.wait_send()

    for k in range(levels):
        sent(spec.at[k], x_send.at[k])
        sent(back.at[k], y_send.at[k])


def correct(base_hbm, planes_hbm, dy_hbm, dx_hbm, upd_hbm, prs_hbm, upd, prs, d_y, d_x, sem, out_sem):
    levels = prs_hbm.shape[0]
    loads = [
        pltpu.make_async_copy(src, dst, sem.at[i])
        for i, (src, dst) in enumerate(
            [(planes_hbm.at[k], prs.at[k]) for k in range(levels)]
            + [
                (dx_hbm, d_x),
                (dy_hbm, d_y),
                (base_hbm.at[pl.ds(0, 2)], upd.at[pl.ds(0, 2)]),
                (planes_hbm.at[levels], prs.at[levels]),
                (base_hbm.at[2], upd.at[2]),
            ]
        )
    ]
    for load in loads:
        load.start()
    for load in loads[: levels + 3]:
        load.wait()
    whole = pltpu.make_async_copy(prs.at[pl.ds(0, levels)], prs_hbm, out_sem.at[levels])
    whole.start()
    outs = []
    uv = pl.ds(0, 2)
    for k in range(levels):
        pressure = prs[k]
        upd[0, k] = upd[0, k] + right_mul(pressure, d_x[0], d_x[1])
        upd[1, k] = upd[1, k] - left_mul(d_y[0], d_y[1], pressure)
        outs.append(pltpu.make_async_copy(upd.at[uv, k], upd_hbm.at[uv, k], out_sem.at[k]))
        outs[-1].start()
    for load in loads[levels + 3 :]:
        load.wait()
    for k in range(levels):
        upd[2, k] = upd[2, k] - (prs[k + 1] - prs[k])
    last = pltpu.make_async_copy(upd.at[2], upd_hbm.at[2], sem.at[levels + 5])
    last.start()
    for copy in (whole, *outs, last):
        copy.wait()


def put(ref, value, n):
    rows = ref.shape[1]
    if rows % 8 == 0:
        ref[...] = value.reshape(ref.shape)
    else:
        for i in range(n):
            ref[i] = value[i * rows : (i + 1) * rows]


def get(ref):
    n, rows, nx = ref.shape
    if rows % 8 == 0:
        return ref[...].reshape(n * rows, nx)
    return jnp.concatenate([ref[i] for i in range(n)], 0)


def local(
    n, groups,
    velocity, fringe_start, turbine_level, turbine_row, turbine_col, thrust, green_basis,
    eigen_shift,
):
    _, _, levels, ny, nx = velocity.shape
    rows = ny // n
    nz = levels * n
    nb = nz * rows
    offset = (np.arange(FRINGE) + 0.5)[:, None]
    ramp_tab = (np.sin(np.pi * offset / FRINGE) ** 2).astype(np.float32)
    hbm = pl.BlockSpec(memory_space=pltpu.HBM)
    smem = pl.BlockSpec(memory_space=pltpu.SMEM)
    plane = (n, rows, nx)
    dma = pltpu.SemaphoreType.DMA
    tabs = [tables(length) for length in ((ny,) if ny == nx else (ny, nx))]
    staged = [
        turbine_level[None], turbine_row[None], turbine_col[None], thrust[None],
        green_basis, eigen_shift[None], ramp_tab, *tabs,
    ]
    fields = velocity[0]
    base, planes = pl.pallas_call(
        functools.partial(kernel, n, groups, len(tabs)),
        out_shape=(
            jax.ShapeDtypeStruct((3, levels, ny, nx), F32),
            jax.ShapeDtypeStruct((levels + 1, ny, nx), F32),
        ),
        in_specs=[hbm, smem] + [hbm] * len(staged),
        out_specs=(hbm, hbm),
        scratch_shapes=[pltpu.VMEM(x.shape, x.dtype) for x in (fields, *staged)]
        + [
            pltpu.VMEM((3, levels, ny, nx), F32),
            pltpu.VMEM((levels, ny, nx), F32),
            pltpu.VMEM((ny, nx), F32),
            pltpu.VMEM((2, ny, nx), F32),
            pltpu.VMEM((2, 2, ny, nx), F32),
            pltpu.VMEM((2, ny, nx), F32),
            pltpu.VMEM((2, ny, nx), F32),
            pltpu.VMEM((2 * levels, FRINGE, ny), F32),
            pltpu.VMEM((2 * levels, FRINGE, ny), F32),
            pltpu.VMEM((levels, *plane), F32),
            pltpu.VMEM((levels, *plane), F32),
            pltpu.VMEM((levels, *plane), F32),
            pltpu.VMEM((levels, *plane), F32),
            pltpu.VMEM((nb, nb), BF16),
            pltpu.VMEM((nb, nb), BF16),
            pltpu.VMEM((nb, nb), BF16),
            pltpu.VMEM((nb, nb), BF16),
            pltpu.VMEM((nb, nx), F32),
            dma((1 + len(staged),)),
            dma((2 + levels,)),
            dma((3, 2)),
            dma((3, 2)),
            dma((max(groups - 1, 1),)),
            dma,
            dma,
            dma,
            dma((levels,)),
            dma((levels,)),
            dma((levels,)),
            dma((levels,)),
        ],
        compiler_params=pltpu.CompilerParams(
            collective_id=0, has_side_effects=True, vmem_limit_bytes=58 * 1024 * 1024
        ),
        name="fractional_step",
    )(fields, fringe_start, *staged)
    derivs = [tab[4:] for tab in tabs]
    updated, pressure = pl.pallas_call(
        correct,
        out_shape=(
            jax.ShapeDtypeStruct((3, levels, ny, nx), F32),
            jax.ShapeDtypeStruct((levels, ny, nx), F32),
        ),
        in_specs=[hbm] * 4,
        out_specs=(hbm, hbm),
        scratch_shapes=[
            pltpu.VMEM((3, levels, ny, nx), F32),
            pltpu.VMEM((levels + 1, ny, nx), F32),
            pltpu.VMEM((2, ny, ny), BF16),
            pltpu.VMEM((2, nx, nx), BF16),
            dma((levels + 6,)),
            dma((levels + 1,)),
        ],
        compiler_params=pltpu.CompilerParams(vmem_limit_bytes=58 * 1024 * 1024),
        name="correction",
    )(base, planes, derivs[0], derivs[-1])
    return updated[None], pressure[None]


def solution(mesh):
    return jax.shard_map(
        functools.partial(local, mesh.shape["gz"], mesh.shape["group"]),
        mesh=mesh,
        in_specs=(P("group", None, "gz", None, None), P(), P(), P(), P(), P(), P(), P()),
        out_specs=(P("group", None, "gz", None, None), P("group", "gz", None, None)),
        check_vma=False,
    )
```

```python
import functools

import jax
import jax.numpy as jnp
import numpy as np
from jax import lax
from jax.experimental import pallas as pl
from jax.experimental.pallas import tpu as pltpu
from jax.sharding import PartitionSpec as P

FRINGE = 32
TIME_STEP = 0.25
MESH = pl.DeviceIdType.MESH
F32 = jnp.float32
BF16 = jnp.bfloat16


def tables(length):
    ids = np.arange(length)
    middle = length // 2
    wave = np.where(ids <= middle, ids, ids - middle)
    phases = 2.0 * np.pi / length * ((wave[:, None] * ids[None, :]) % length)
    norm = np.sqrt(np.where((ids == 0) | (ids == middle), 1.0, 2.0) / length)[:, None]
    basis = np.where(ids[:, None] <= middle, np.cos(phases), np.sin(phases)) * norm
    coupling = np.zeros((length, length))
    inner = np.arange(1, middle)
    coupling[inner, inner + middle] = 2.0 * np.pi * inner / length
    coupling[inner + middle, inner] = -2.0 * np.pi * inner / length
    deriv = basis.T @ coupling @ basis
    deriv = 0.5 * (deriv - deriv.T)
    parts = []
    for matrix in (basis, basis.T, deriv):
        whole = matrix.astype(np.float32)
        high = whole.astype(jnp.bfloat16)
        parts += [high, (whole - high.astype(np.float32)).astype(jnp.bfloat16)]
    return np.stack(parts)


def split(value):
    high = value.astype(BF16)
    return high, (value - high.astype(F32)).astype(BF16)


def dot(left, right):
    return jnp.dot(left, right, preferred_element_type=F32)


def dot_nt(left, right):
    return lax.dot_general(left, right, (((1,), (1,)), ((), ())), preferred_element_type=F32)


def left_mul(high, low, value):
    vh, vl = split(value)
    return dot(jnp.concatenate([high, high, low], 1), jnp.concatenate([vh, vl, vh], 0))


def right_mul(value, high, low):
    vh, vl = split(value)
    return dot(jnp.concatenate([vh, vl, vh], 1), jnp.concatenate([high, high, low], 0))


def iota(shape, dim):
    return lax.broadcasted_iota(jnp.int32, shape, dim)


def onehot(hit):
    return jnp.where(hit, 1.0, 0.0).astype(BF16)


def kernel(
    n, groups, tab_count,
    vel_hbm, start_ref, *refs,
):
    staged = refs[: 7 + tab_count]
    upd_hbm, prs_hbm = refs[7 + tab_count : 9 + tab_count]
    vel = refs[9 + tab_count]
    local_refs = refs[10 + tab_count : 17 + 2 * tab_count]
    tlevel, trow, tcol, thrust, green, shift, ramp_tab = local_refs[:7]
    tab_y, tab_x = local_refs[7], local_refs[-1]
    (
        upd, prs, p_above, w_side, uv_side, h_src, h_side, fr_src, fr_buf,
        spec, modes, back, planes, m_hi, m_lo, mt_hi, mt_lo, inv,
        in_sem, out_sem, halo_send, halo_recv, fr_send, fr_recv, pa_send, pa_recv,
        x_send, x_recv, y_send, y_recv,
    ) = refs[17 + 2 * tab_count :]
    levels, ny, nx = vel.shape[1:]
    rows = ny // n
    nz = levels * n
    nb = nz * rows
    me = lax.axis_index("gz")
    group = lax.axis_index("group")
    up = lax.rem(me + 1, n)
    down = lax.rem(me + n - 1, n)
    top = levels - 1

    loads = [
        pltpu.make_async_copy(src, dst, in_sem.at[i])
        for i, (src, dst) in enumerate(zip((vel_hbm, *staged), (vel, *local_refs)))
    ]
    loads[0].start()
    barrier = pltpu.get_barrier_semaphore()

    @pl.loop(1, n)
    def _(off):
        pl.semaphore_signal(
            barrier, inc=1, device_id={"gz": lax.rem(me + off, n)}, device_id_type=MESH
        )

    for off in range(1, groups):
        pl.semaphore_signal(
            barrier, inc=1, device_id={"group": lax.rem(group + off, groups)}, device_id_type=MESH
        )
    for load in loads[1:]:
        load.start()
    loads[0].wait()
    pl.semaphore_wait(barrier, n - 1 + groups - 1)

    def remote(src, dst, send, recv, where):
        return pltpu.make_async_remote_copy(
            src_ref=src, dst_ref=dst, send_sem=send, recv_sem=recv,
            device_id=where, device_id_type=MESH,
        )

    inner = 1 - lax.rem(me, 2)
    outer = 1 - inner

    def there(side):
        return jnp.where(side == 1, me < n - 1, me > 0)

    def toward(side):
        return jnp.where(side == 1, up, down)

    uv = pl.ds(0, 2)

    def halo(src, dst, kind, side):
        return remote(
            src, dst.at[1 - side], halo_send.at[kind, side], halo_recv.at[kind, 1 - side],
            {"gz": toward(side)},
        )

    def halo_copy(kind, side):
        if kind == 0:
            return halo(vel.at[2, side * top], w_side, kind, side)
        if kind == 1:
            return halo(h_src.at[side], h_side, kind, side)
        return halo(vel.at[uv, side * top], uv_side, kind, side)

    def send(kind, side):
        @pl.when(there(side))
        def _():
            halo_copy(kind, side).start()

    def receive(kind, side):
        @pl.when(there(side))
        def _():
            halo_copy(kind, 1 - side).wait_recv()

    send(0, inner)
    send(0, outer)

    for side in range(2):

        @pl.when(jnp.logical_not(there(side)))
        def _():
            w_side[side] = jnp.zeros((ny, nx), F32)
            h_side[side] = jnp.zeros((ny, nx), F32)
            uv_side[side] = jnp.zeros((2, ny, nx), F32)

    for load in loads[1:]:
        load.wait()

    start = start_ref[0]
    pick = iota((FRINGE, nx), 1) - start == iota((FRINGE, nx), 0)
    pick_b = onehot(pick)
    fringe_copies = [
        remote(fr_src, fr_buf, fr_send.at[g - 1], fr_recv, {"group": g}) for g in range(1, groups)
    ]

    @pl.when(group == 0)
    def _():
        fr_buf[...] = jnp.zeros_like(fr_buf)
        for c in range(2):
            for k in range(levels):
                vh, vl = split(vel[c, k])
                fr_src[c * levels + k] = dot_nt(pick_b, vh) + dot_nt(pick_b, vl)
        for copy in fringe_copies:
            copy.start()

    is_farm = jnp.where(group > 0, 1.0, 0.0)
    ramp = is_farm * jnp.sum(jnp.where(pick, ramp_tab[...], 0.0), axis=0, keepdims=True)
    keep = 1.0 - ramp

    r_y = (tab_y[0], tab_y[1])
    rt_y = (tab_y[2], tab_y[3])
    d_y = (tab_y[4], tab_y[5])
    r_x = (tab_x[0], tab_x[1])
    rt_x = (tab_x[2], tab_x[3])
    d_x = (tab_x[4], tab_x[5])

    def dx(value):
        return -right_mul(value, *d_x)

    def dy(value):
        return left_mul(*d_y, value)

    turbines = trow.shape[1]
    pick_row = iota((ny, turbines), 0) == trow[...]
    pick_col = onehot(iota((nx, turbines), 0) == tcol[...])

    def predict(c, k):
        field = vel[c, k]
        if k < top and k > 0:
            vertical = vel[c, k + 1] - vel[c, k - 1]
        elif k < top:
            vertical = vel[c, k + 1]
        elif k > 0:
            vertical = -vel[c, k - 1]
        else:
            vertical = jnp.zeros_like(field)
        tend = -(vel[0, k] * dx(field) + vel[1, k] * dy(field) + (0.5 * vel[2, k]) * vertical)
        upd[c, k] = field + TIME_STEP * tend

    for k in range(levels):
        for c in (2, 0, 1):
            predict(c, k)

    half = 0.5 * TIME_STEP

    for side in (inner, outer):
        signed = half * (2 * side - 1).astype(F32)
        edge = side * top
        receive(0, side)
        w_there = w_side[side]
        upd[2, edge] = upd[2, edge] - signed * (vel[2, edge] * w_there)
        weight = (signed * keep) * w_there
        h_src[side] = (
            dx(weight * vel[0, edge])
            + dy(weight * vel[1, edge])
            - side.astype(F32) * upd[2, top]
        )
        send(1, side)

    speed = jnp.zeros((1, turbines), F32)
    for k in range(levels):
        vh, vl = split(vel[0, k])
        at_col = dot(vh, pick_col) + dot(vl, pick_col)
        here = jnp.sum(jnp.where(pick_row, at_col, 0.0), axis=0, keepdims=True)
        speed = speed + jnp.where(tlevel[...] == me * levels + k, here, 0.0)
    drag = (-TIME_STEP * is_farm) * thrust[...] * jnp.abs(speed) * speed
    for k in range(levels):
        placed = jnp.where(pick_row & (tlevel[...] == me * levels + k), drag, 0.0)
        ph, pw = split(placed)
        upd[0, k] = upd[0, k] + dot_nt(ph, pick_col) + dot_nt(pw, pick_col)

    @pl.when(group > 0)
    def _():
        fringe_copies[0].wait_recv()

    for k in range(levels):
        for c in range(2):
            th, tl = split(fr_buf[c * levels + k].T)
            upstream = dot(th, pick_b) + dot(tl, pick_b)
            predicted = upd[c, k]
            upd[c, k] = predicted + ramp * (upstream - predicted)

    for k in range(levels):
        divergence = dx(upd[0, k]) + dy(upd[1, k]) + upd[2, k]
        if k > 0:
            divergence = divergence - upd[2, k - 1]
        prs[k] = divergence

    def exchange(src, dst, send, recv):
        pltpu.make_async_copy(src.at[me], dst.at[me], recv).start()

        @pl.loop(0, n - 1)
        def _(i):
            odd = lax.rem(i, 2)
            peer = lax.rem(me + n // 2 + (1 - 2 * odd) * ((i + 1) // 2), n)
            remote(src.at[peer], dst.at[me], send, recv, {"gz": peer}).start()

    def arrived(dst, recv):
        pltpu.make_async_copy(dst, dst, recv).wait()

    def sent(src, send):
        most = src.at[pl.ds(0, n - 1)]
        pltpu.make_async_copy(most, most, send).wait()

    def transform(k):
        put(spec.at[k], right_mul(left_mul(*r_y, prs[k]), *rt_x), n)
        exchange(spec.at[k], modes.at[k], x_send.at[k], x_recv.at[k])

    for side in (inner, outer):
        edge = side * top
        receive(1, side)
        prs[edge] = prs[edge] + h_side[side]
        transform(edge)
    for k in range(1, top):
        transform(k)
    send(2, 1)

    rbits = rows.bit_length() - 1
    ybits = ny.bit_length() - 1
    eig = iota((nb, nz), 0) >> rbits == iota((nb, nz), 1)
    pos = iota((nb, nz), 0)
    lev = ((pos & (ny - 1)) >> rbits) * levels + (pos >> ybits) == iota((nb, nz), 1)
    eig_b, lev_b = onehot(eig), onehot(lev)
    same = (iota((nb, nb), 0) & (rows - 1)) == (iota((nb, nb), 1) & (rows - 1))
    for part, to, to_t in zip(split(green[...]), (m_hi, m_lo), (mt_hi, mt_lo)):
        wide = dot(eig_b, part).astype(BF16)
        to[...] = jnp.where(same, dot_nt(wide, lev_b), 0.0).astype(BF16)
        wide_t = dot_nt(lev_b, part).astype(BF16)
        to_t[...] = jnp.where(same, dot_nt(wide_t, eig_b), 0.0).astype(BF16)
    shifts = jnp.sum(jnp.where(eig, shift[...], 0.0), axis=1, keepdims=True)

    def wave_square(ids, length):
        wave = jnp.where(ids <= length // 2, ids, ids - length // 2)
        wave = wave.astype(F32) * (2.0 * np.pi / length)
        return wave * wave

    ky = me * rows + (iota((nb, 1), 0) & (rows - 1))
    kx = iota((1, nx), 1)
    inv[...] = 1.0 / (shifts + (wave_square(ky, ny) + wave_square(kx, nx)))

    scaled = None
    for k in range(top, -1, -1):
        arrived(modes.at[k], x_recv.at[k])
        cols = pl.ds(k * ny, ny)
        term = left_mul(m_hi[:, cols], m_lo[:, cols], get(modes.at[k]))
        scaled = term if scaled is None else scaled + term
    send(2, 0)
    scaled = scaled * inv[...]
    for k in range(levels):
        own = pl.ds(k * ny, ny)
        put(back.at[k], left_mul(mt_hi[own], mt_lo[own], scaled), n)
        exchange(back.at[k], planes.at[k], y_send.at[k], y_recv.at[k])
    for side in range(2):
        edge = side * top
        signed = half * (2 * side - 1)
        receive(2, side)
        for c in range(2):
            upd[c, edge] = upd[c, edge] - (signed * keep) * (vel[2, edge] * uv_side[side, c])
    out_upd = pltpu.make_async_copy(upd, upd_hbm, out_sem.at[0])
    out_upd.start()

    p_down = remote(prs.at[0], p_above, pa_send, pa_recv, {"gz": down})

    @pl.when(jnp.logical_not(there(1)))
    def _():
        p_above[...] = jnp.zeros((ny, nx), F32)

    out_prs = []
    for k in range(levels):
        arrived(planes.at[k], y_recv.at[k])
        prs[k] = right_mul(left_mul(*rt_y, get(planes.at[k])), *r_x)
        if k == 0:

            @pl.when(there(0))
            def _():
                p_down.start()

        copy = pltpu.make_async_copy(prs.at[k], prs_hbm.at[k], out_sem.at[2 + k])
        copy.start()
        out_prs.append(copy)

    @pl.when(there(1))
    def _():
        p_down.wait_recv()

    out_above = pltpu.make_async_copy(p_above, prs_hbm.at[levels], out_sem.at[1])
    out_above.start()
    out_upd.wait()
    for copy in out_prs:
        copy.wait()
    out_above.wait()

    for side in range(2):

        @pl.when(there(side))
        def _():
            for kind in range(3):
                halo_copy(kind, side).wait_send()

    @pl.when(there(0))
    def _():
        p_down.wait_send()

    @pl.when(group == 0)
    def _():
        for copy in fringe_copies:
            copy.wait_send()

    for k in range(levels):
        sent(spec.at[k], x_send.at[k])
        sent(back.at[k], y_send.at[k])


def correct(base_hbm, planes_hbm, dy_hbm, dx_hbm, upd_hbm, prs_hbm, upd, prs, d_y, d_x, sem, out_sem):
    levels = prs_hbm.shape[0]
    loads = [
        pltpu.make_async_copy(src, dst, sem.at[i])
        for i, (src, dst) in enumerate(
            [(planes_hbm.at[k], prs.at[k]) for k in range(levels)]
            + [
                (dx_hbm, d_x),
                (dy_hbm, d_y),
                (base_hbm.at[pl.ds(0, 2)], upd.at[pl.ds(0, 2)]),
                (planes_hbm.at[levels], prs.at[levels]),
                (base_hbm.at[2], upd.at[2]),
            ]
        )
    ]
    for load in loads:
        load.start()
    for load in loads[: levels + 3]:
        load.wait()
    whole = pltpu.make_async_copy(prs.at[pl.ds(0, levels)], prs_hbm, out_sem.at[levels])
    whole.start()
    outs = []
    uv = pl.ds(0, 2)
    for k in range(levels):
        pressure = prs[k]
        upd[0, k] = upd[0, k] + right_mul(pressure, d_x[0], d_x[1])
        upd[1, k] = upd[1, k] - left_mul(d_y[0], d_y[1], pressure)
        outs.append(pltpu.make_async_copy(upd.at[uv, k], upd_hbm.at[uv, k], out_sem.at[k]))
        outs[-1].start()
    for load in loads[levels + 3 :]:
        load.wait()
    for k in range(levels):
        upd[2, k] = upd[2, k] - (prs[k + 1] - prs[k])
    last = pltpu.make_async_copy(upd.at[2], upd_hbm.at[2], sem.at[levels + 5])
    last.start()
    for copy in (whole, *outs, last):
        copy.wait()


def put(ref, value, n):
    rows = ref.shape[1]
    if rows % 8 == 0:
        ref[...] = value.reshape(ref.shape)
    else:
        for i in range(n):
            ref[i] = value[i * rows : (i + 1) * rows]


def get(ref):
    n, rows, nx = ref.shape
    if rows % 8 == 0:
        return ref[...].reshape(n * rows, nx)
    return jnp.concatenate([ref[i] for i in range(n)], 0)


def local(
    n, groups,
    velocity, fringe_start, turbine_level, turbine_row, turbine_col, thrust, green_basis,
    eigen_shift,
):
    _, _, levels, ny, nx = velocity.shape
    rows = ny // n
    nz = levels * n
    nb = nz * rows
    offset = (np.arange(FRINGE) + 0.5)[:, None]
    ramp_tab = (np.sin(np.pi * offset / FRINGE) ** 2).astype(np.float32)
    hbm = pl.BlockSpec(memory_space=pltpu.HBM)
    smem = pl.BlockSpec(memory_space=pltpu.SMEM)
    plane = (n, rows, nx)
    dma = pltpu.SemaphoreType.DMA
    tabs = [tables(length) for length in ((ny,) if ny == nx else (ny, nx))]
    staged = [
        turbine_level[None], turbine_row[None], turbine_col[None], thrust[None],
        green_basis, eigen_shift[None], ramp_tab, *tabs,
    ]
    fields = velocity[0]
    base, planes = pl.pallas_call(
        functools.partial(kernel, n, groups, len(tabs)),
        out_shape=(
            jax.ShapeDtypeStruct((3, levels, ny, nx), F32),
            jax.ShapeDtypeStruct((levels + 1, ny, nx), F32),
        ),
        in_specs=[hbm, smem] + [hbm] * len(staged),
        out_specs=(hbm, hbm),
        scratch_shapes=[pltpu.VMEM(x.shape, x.dtype) for x in (fields, *staged)]
        + [
            pltpu.VMEM((3, levels, ny, nx), F32),
            pltpu.VMEM((levels, ny, nx), F32),
            pltpu.VMEM((ny, nx), F32),
            pltpu.VMEM((2, ny, nx), F32),
            pltpu.VMEM((2, 2, ny, nx), F32),
            pltpu.VMEM((2, ny, nx), F32),
            pltpu.VMEM((2, ny, nx), F32),
            pltpu.VMEM((2 * levels, FRINGE, ny), F32),
            pltpu.VMEM((2 * levels, FRINGE, ny), F32),
            pltpu.VMEM((levels, *plane), F32),
            pltpu.VMEM((levels, *plane), F32),
            pltpu.VMEM((levels, *plane), F32),
            pltpu.VMEM((levels, *plane), F32),
            pltpu.VMEM((nb, nb), BF16),
            pltpu.VMEM((nb, nb), BF16),
            pltpu.VMEM((nb, nb), BF16),
            pltpu.VMEM((nb, nb), BF16),
            pltpu.VMEM((nb, nx), F32),
            dma((1 + len(staged),)),
            dma((2 + levels,)),
            dma((3, 2)),
            dma((3, 2)),
            dma((max(groups - 1, 1),)),
            dma,
            dma,
            dma,
            dma((levels,)),
            dma((levels,)),
            dma((levels,)),
            dma((levels,)),
        ],
        compiler_params=pltpu.CompilerParams(
            collective_id=0, has_side_effects=True, vmem_limit_bytes=58 * 1024 * 1024
        ),
        name="fractional_step",
    )(fields, fringe_start, *staged)
    derivs = [tab[4:] for tab in tabs]
    updated, pressure = pl.pallas_call(
        correct,
        out_shape=(
            jax.ShapeDtypeStruct((3, levels, ny, nx), F32),
            jax.ShapeDtypeStruct((levels, ny, nx), F32),
        ),
        in_specs=[hbm] * 4,
        out_specs=(hbm, hbm),
        scratch_shapes=[
            pltpu.VMEM((3, levels, ny, nx), F32),
            pltpu.VMEM((levels + 1, ny, nx), F32),
            pltpu.VMEM((2, ny, ny), BF16),
            pltpu.VMEM((2, nx, nx), BF16),
            dma((levels + 6,)),
            dma((levels + 1,)),
        ],
        compiler_params=pltpu.CompilerParams(vmem_limit_bytes=58 * 1024 * 1024),
        name="correction",
    )(base, planes, derivs[0], derivs[-1])
    return updated[None], pressure[None]


def solution(mesh):
    return jax.shard_map(
        functools.partial(local, mesh.shape["gz"], mesh.shape["group"]),
        mesh=mesh,
        in_specs=(P("group", None, "gz", None, None), P(), P(), P(), P(), P(), P(), P()),
        out_specs=(P("group", None, "gz", None, None), P("group", "gz", None, None)),
        check_vma=False,
    )
```

```python
import functools

import jax
import jax.numpy as jnp
import numpy as np
from jax import lax
from jax.experimental import pallas as pl
from jax.experimental.pallas import tpu as pltpu
from jax.sharding import PartitionSpec as P

FRINGE = 32
TIME_STEP = 0.25
MESH = pl.DeviceIdType.MESH
F32 = jnp.float32
BF16 = jnp.bfloat16


def tables(length):
    ids = np.arange(length)
    middle = length // 2
    wave = np.where(ids <= middle, ids, ids - middle)
    phases = 2.0 * np.pi / length * ((wave[:, None] * ids[None, :]) % length)
    norm = np.sqrt(np.where((ids == 0) | (ids == middle), 1.0, 2.0) / length)[:, None]
    basis = np.where(ids[:, None] <= middle, np.cos(phases), np.sin(phases)) * norm
    coupling = np.zeros((length, length))
    inner = np.arange(1, middle)
    coupling[inner, inner + middle] = 2.0 * np.pi * inner / length
    coupling[inner + middle, inner] = -2.0 * np.pi * inner / length
    deriv = basis.T @ coupling @ basis
    deriv = 0.5 * (deriv - deriv.T)
    parts = []
    for matrix in (basis, basis.T, deriv):
        whole = matrix.astype(np.float32)
        high = whole.astype(jnp.bfloat16)
        parts += [high, (whole - high.astype(np.float32)).astype(jnp.bfloat16)]
    return np.stack(parts)


def split(value):
    high = value.astype(BF16)
    return high, (value - high.astype(F32)).astype(BF16)


def dot(left, right):
    return jnp.dot(left, right, preferred_element_type=F32)


def dot_nt(left, right):
    return lax.dot_general(left, right, (((1,), (1,)), ((), ())), preferred_element_type=F32)


def left_mul(high, low, value):
    vh, vl = split(value)
    return dot(jnp.concatenate([high, high, low], 1), jnp.concatenate([vh, vl, vh], 0))


def right_mul(value, high, low):
    vh, vl = split(value)
    return dot(jnp.concatenate([vh, vl, vh], 1), jnp.concatenate([high, high, low], 0))


def iota(shape, dim):
    return lax.broadcasted_iota(jnp.int32, shape, dim)


def onehot(hit):
    return jnp.where(hit, 1.0, 0.0).astype(BF16)


def kernel(
    n, groups, tab_count,
    vel_hbm, start_ref, *refs,
):
    staged = refs[: 7 + tab_count]
    upd_hbm, prs_hbm = refs[7 + tab_count : 9 + tab_count]
    vel = refs[9 + tab_count]
    local_refs = refs[10 + tab_count : 17 + 2 * tab_count]
    tlevel, trow, tcol, thrust, green, shift, ramp_tab = local_refs[:7]
    tab_y, tab_x = local_refs[7], local_refs[-1]
    (
        upd, prs, p_above, w_side, uv_side, h_src, h_side, fr_src, fr_buf,
        spec, modes, back, planes, m_hi, m_lo, mt_hi, mt_lo, inv,
        in_sem, out_sem, halo_send, halo_recv, fr_send, fr_recv, pa_send, pa_recv,
        x_send, x_recv, y_send, y_recv,
    ) = refs[17 + 2 * tab_count :]
    levels, ny, nx = vel.shape[1:]
    rows = ny // n
    nz = levels * n
    nb = nz * rows
    me = lax.axis_index("gz")
    group = lax.axis_index("group")
    up = lax.rem(me + 1, n)
    down = lax.rem(me + n - 1, n)
    top = levels - 1

    loads = [
        pltpu.make_async_copy(src, dst, in_sem.at[i])
        for i, (src, dst) in enumerate(zip((vel_hbm, *staged), (vel, *local_refs)))
    ]
    loads[0].start()
    barrier = pltpu.get_barrier_semaphore()

    @pl.loop(1, n)
    def _(off):
        pl.semaphore_signal(
            barrier, inc=1, device_id={"gz": lax.rem(me + off, n)}, device_id_type=MESH
        )

    for off in range(1, groups):
        pl.semaphore_signal(
            barrier, inc=1, device_id={"group": lax.rem(group + off, groups)}, device_id_type=MESH
        )
    for load in loads[1:]:
        load.start()
    loads[0].wait()
    pl.semaphore_wait(barrier, n - 1 + groups - 1)

    def remote(src, dst, send, recv, where):
        return pltpu.make_async_remote_copy(
            src_ref=src, dst_ref=dst, send_sem=send, recv_sem=recv,
            device_id=where, device_id_type=MESH,
        )

    inner = 1 - lax.rem(me, 2)
    outer = 1 - inner

    def there(side):
        return jnp.where(side == 1, me < n - 1, me > 0)

    def toward(side):
        return jnp.where(side == 1, up, down)

    uv = pl.ds(0, 2)

    def halo(src, dst, kind, side):
        return remote(
            src, dst.at[1 - side], halo_send.at[kind, side], halo_recv.at[kind, 1 - side],
            {"gz": toward(side)},
        )

    def halo_copy(kind, side):
        if kind == 0:
            return halo(vel.at[2, side * top], w_side, kind, side)
        if kind == 1:
            return halo(h_src.at[side], h_side, kind, side)
        return halo(vel.at[uv, side * top], uv_side, kind, side)

    def send(kind, side):
        @pl.when(there(side))
        def _():
            halo_copy(kind, side).start()

    def receive(kind, side):
        @pl.when(there(side))
        def _():
            halo_copy(kind, 1 - side).wait_recv()

    send(0, inner)
    send(0, outer)

    for side in range(2):

        @pl.when(jnp.logical_not(there(side)))
        def _():
            w_side[side] = jnp.zeros((ny, nx), F32)
            h_side[side] = jnp.zeros((ny, nx), F32)
            uv_side[side] = jnp.zeros((2, ny, nx), F32)

    for load in loads[1:]:
        load.wait()

    start = start_ref[0]
    pick = iota((FRINGE, nx), 1) - start == iota((FRINGE, nx), 0)
    pick_b = onehot(pick)
    fringe_copies = [
        remote(fr_src, fr_buf, fr_send.at[g - 1], fr_recv, {"group": g}) for g in range(1, groups)
    ]

    @pl.when(group == 0)
    def _():
        fr_buf[...] = jnp.zeros_like(fr_buf)
        for c in range(2):
            for k in range(levels):
                vh, vl = split(vel[c, k])
                fr_src[c * levels + k] = dot_nt(pick_b, vh) + dot_nt(pick_b, vl)
        for copy in fringe_copies:
            copy.start()

    is_farm = jnp.where(group > 0, 1.0, 0.0)
    ramp = is_farm * jnp.sum(jnp.where(pick, ramp_tab[...], 0.0), axis=0, keepdims=True)
    keep = 1.0 - ramp

    r_y = (tab_y[0], tab_y[1])
    rt_y = (tab_y[2], tab_y[3])
    d_y = (tab_y[4], tab_y[5])
    r_x = (tab_x[0], tab_x[1])
    rt_x = (tab_x[2], tab_x[3])
    d_x = (tab_x[4], tab_x[5])

    def dx(value):
        return -right_mul(value, *d_x)

    def dy(value):
        return left_mul(*d_y, value)

    turbines = trow.shape[1]
    pick_row = iota((ny, turbines), 0) == trow[...]
    pick_col = onehot(iota((nx, turbines), 0) == tcol[...])

    def predict(c, k):
        field = vel[c, k]
        if k < top and k > 0:
            vertical = vel[c, k + 1] - vel[c, k - 1]
        elif k < top:
            vertical = vel[c, k + 1]
        elif k > 0:
            vertical = -vel[c, k - 1]
        else:
            vertical = jnp.zeros_like(field)
        tend = -(vel[0, k] * dx(field) + vel[1, k] * dy(field) + (0.5 * vel[2, k]) * vertical)
        upd[c, k] = field + TIME_STEP * tend

    for k in range(levels):
        for c in (2, 0, 1):
            predict(c, k)

    half = 0.5 * TIME_STEP

    for side in (inner, outer):
        signed = half * (2 * side - 1).astype(F32)
        edge = side * top
        receive(0, side)
        w_there = w_side[side]
        upd[2, edge] = upd[2, edge] - signed * (vel[2, edge] * w_there)
        weight = (signed * keep) * w_there
        h_src[side] = (
            dx(weight * vel[0, edge])
            + dy(weight * vel[1, edge])
            - side.astype(F32) * upd[2, top]
        )
        send(1, side)

    speed = jnp.zeros((1, turbines), F32)
    for k in range(levels):
        vh, vl = split(vel[0, k])
        at_col = dot(vh, pick_col) + dot(vl, pick_col)
        here = jnp.sum(jnp.where(pick_row, at_col, 0.0), axis=0, keepdims=True)
        speed = speed + jnp.where(tlevel[...] == me * levels + k, here, 0.0)
    drag = (-TIME_STEP * is_farm) * thrust[...] * jnp.abs(speed) * speed
    for k in range(levels):
        placed = jnp.where(pick_row & (tlevel[...] == me * levels + k), drag, 0.0)
        ph, pw = split(placed)
        upd[0, k] = upd[0, k] + dot_nt(ph, pick_col) + dot_nt(pw, pick_col)

    @pl.when(group > 0)
    def _():
        fringe_copies[0].wait_recv()

    for k in range(levels):
        for c in range(2):
            th, tl = split(fr_buf[c * levels + k].T)
            upstream = dot(th, pick_b) + dot(tl, pick_b)
            predicted = upd[c, k]
            upd[c, k] = predicted + ramp * (upstream - predicted)

    for k in range(levels):
        divergence = dx(upd[0, k]) + dy(upd[1, k]) + upd[2, k]
        if k > 0:
            divergence = divergence - upd[2, k - 1]
        prs[k] = divergence

    flips = [2**bit * (1 - 2 * lax.rem(me // 2**bit, 2)) for bit in range(n.bit_length() - 1)]

    def exchange(src, dst, send, recv):
        pltpu.make_async_copy(src.at[me], dst.at[me], recv).start()

        @pl.loop(0, n - 1)
        def _(i):
            odd = lax.rem(i, 2)
            mask = (1 - odd) * (n // 2 + i // 2) + odd * ((i + 1) // 2)
            peer = me
            for bit, flip in enumerate(flips):
                peer = peer + lax.rem(mask // 2**bit, 2) * flip
            remote(src.at[peer], dst.at[me], send, recv, {"gz": peer}).start()

    def arrived(dst, recv):
        pltpu.make_async_copy(dst, dst, recv).wait()

    def sent(src, send):
        most = src.at[pl.ds(0, n - 1)]
        pltpu.make_async_copy(most, most, send).wait()

    def transform(k):
        put(spec.at[k], right_mul(left_mul(*r_y, prs[k]), *rt_x), n)
        exchange(spec.at[k], modes.at[k], x_send.at[k], x_recv.at[k])

    for side in (inner, outer):
        edge = side * top
        receive(1, side)
        prs[edge] = prs[edge] + h_side[side]
        transform(edge)
    for k in range(1, top):
        transform(k)
    send(2, 1)

    rbits = rows.bit_length() - 1
    ybits = ny.bit_length() - 1
    eig = iota((nb, nz), 0) >> rbits == iota((nb, nz), 1)
    pos = iota((nb, nz), 0)
    lev = ((pos & (ny - 1)) >> rbits) * levels + (pos >> ybits) == iota((nb, nz), 1)
    eig_b, lev_b = onehot(eig), onehot(lev)
    same = (iota((nb, nb), 0) & (rows - 1)) == (iota((nb, nb), 1) & (rows - 1))
    for part, to, to_t in zip(split(green[...]), (m_hi, m_lo), (mt_hi, mt_lo)):
        wide = dot(eig_b, part).astype(BF16)
        to[...] = jnp.where(same, dot_nt(wide, lev_b), 0.0).astype(BF16)
        wide_t = dot_nt(lev_b, part).astype(BF16)
        to_t[...] = jnp.where(same, dot_nt(wide_t, eig_b), 0.0).astype(BF16)
    shifts = jnp.sum(jnp.where(eig, shift[...], 0.0), axis=1, keepdims=True)

    def wave_square(ids, length):
        wave = jnp.where(ids <= length // 2, ids, ids - length // 2)
        wave = wave.astype(F32) * (2.0 * np.pi / length)
        return wave * wave

    ky = me * rows + (iota((nb, 1), 0) & (rows - 1))
    kx = iota((1, nx), 1)
    inv[...] = 1.0 / (shifts + (wave_square(ky, ny) + wave_square(kx, nx)))

    scaled = None
    for k in range(top, -1, -1):
        arrived(modes.at[k], x_recv.at[k])
        cols = pl.ds(k * ny, ny)
        term = left_mul(m_hi[:, cols], m_lo[:, cols], get(modes.at[k]))
        scaled = term if scaled is None else scaled + term
    send(2, 0)
    scaled = scaled * inv[...]
    for k in range(levels):
        own = pl.ds(k * ny, ny)
        put(back.at[k], left_mul(mt_hi[own], mt_lo[own], scaled), n)
        exchange(back.at[k], planes.at[k], y_send.at[k], y_recv.at[k])
    for side in range(2):
        edge = side * top
        signed = half * (2 * side - 1)
        receive(2, side)
        for c in range(2):
            upd[c, edge] = upd[c, edge] - (signed * keep) * (vel[2, edge] * uv_side[side, c])
    out_upd = pltpu.make_async_copy(upd, upd_hbm, out_sem.at[0])
    out_upd.start()

    p_down = remote(prs.at[0], p_above, pa_send, pa_recv, {"gz": down})

    @pl.when(jnp.logical_not(there(1)))
    def _():
        p_above[...] = jnp.zeros((ny, nx), F32)

    out_prs = []
    for k in range(levels):
        arrived(planes.at[k], y_recv.at[k])
        prs[k] = right_mul(left_mul(*rt_y, get(planes.at[k])), *r_x)
        if k == 0:

            @pl.when(there(0))
            def _():
                p_down.start()

        copy = pltpu.make_async_copy(prs.at[k], prs_hbm.at[k], out_sem.at[2 + k])
        copy.start()
        out_prs.append(copy)

    @pl.when(there(1))
    def _():
        p_down.wait_recv()

    out_above = pltpu.make_async_copy(p_above, prs_hbm.at[levels], out_sem.at[1])
    out_above.start()
    out_upd.wait()
    for copy in out_prs:
        copy.wait()
    out_above.wait()

    for side in range(2):

        @pl.when(there(side))
        def _():
            for kind in range(3):
                halo_copy(kind, side).wait_send()

    @pl.when(there(0))
    def _():
        p_down.wait_send()

    @pl.when(group == 0)
    def _():
        for copy in fringe_copies:
            copy.wait_send()

    for k in range(levels):
        sent(spec.at[k], x_send.at[k])
        sent(back.at[k], y_send.at[k])


def correct(base_hbm, planes_hbm, dy_hbm, dx_hbm, upd_hbm, prs_hbm, upd, prs, d_y, d_x, sem, out_sem):
    levels = prs_hbm.shape[0]
    loads = [
        pltpu.make_async_copy(src, dst, sem.at[i])
        for i, (src, dst) in enumerate(
            [(planes_hbm.at[k], prs.at[k]) for k in range(levels)]
            + [
                (dx_hbm, d_x),
                (dy_hbm, d_y),
                (base_hbm.at[pl.ds(0, 2)], upd.at[pl.ds(0, 2)]),
                (planes_hbm.at[levels], prs.at[levels]),
                (base_hbm.at[2], upd.at[2]),
            ]
        )
    ]
    for load in loads:
        load.start()
    for load in loads[: levels + 3]:
        load.wait()
    whole = pltpu.make_async_copy(prs.at[pl.ds(0, levels)], prs_hbm, out_sem.at[levels])
    whole.start()
    outs = []
    uv = pl.ds(0, 2)
    for k in range(levels):
        pressure = prs[k]
        upd[0, k] = upd[0, k] + right_mul(pressure, d_x[0], d_x[1])
        upd[1, k] = upd[1, k] - left_mul(d_y[0], d_y[1], pressure)
        outs.append(pltpu.make_async_copy(upd.at[uv, k], upd_hbm.at[uv, k], out_sem.at[k]))
        outs[-1].start()
    for load in loads[levels + 3 :]:
        load.wait()
    for k in range(levels):
        upd[2, k] = upd[2, k] - (prs[k + 1] - prs[k])
    last = pltpu.make_async_copy(upd.at[2], upd_hbm.at[2], sem.at[levels + 5])
    last.start()
    for copy in (whole, *outs, last):
        copy.wait()


def put(ref, value, n):
    rows = ref.shape[1]
    if rows % 8 == 0:
        ref[...] = value.reshape(ref.shape)
    else:
        for i in range(n):
            ref[i] = value[i * rows : (i + 1) * rows]


def get(ref):
    n, rows, nx = ref.shape
    if rows % 8 == 0:
        return ref[...].reshape(n * rows, nx)
    return jnp.concatenate([ref[i] for i in range(n)], 0)


def local(
    n, groups,
    velocity, fringe_start, turbine_level, turbine_row, turbine_col, thrust, green_basis,
    eigen_shift,
):
    _, _, levels, ny, nx = velocity.shape
    rows = ny // n
    nz = levels * n
    nb = nz * rows
    offset = (np.arange(FRINGE) + 0.5)[:, None]
    ramp_tab = (np.sin(np.pi * offset / FRINGE) ** 2).astype(np.float32)
    hbm = pl.BlockSpec(memory_space=pltpu.HBM)
    smem = pl.BlockSpec(memory_space=pltpu.SMEM)
    plane = (n, rows, nx)
    dma = pltpu.SemaphoreType.DMA
    tabs = [tables(length) for length in ((ny,) if ny == nx else (ny, nx))]
    staged = [
        turbine_level[None], turbine_row[None], turbine_col[None], thrust[None],
        green_basis, eigen_shift[None], ramp_tab, *tabs,
    ]
    fields = velocity[0]
    base, planes = pl.pallas_call(
        functools.partial(kernel, n, groups, len(tabs)),
        out_shape=(
            jax.ShapeDtypeStruct((3, levels, ny, nx), F32),
            jax.ShapeDtypeStruct((levels + 1, ny, nx), F32),
        ),
        in_specs=[hbm, smem] + [hbm] * len(staged),
        out_specs=(hbm, hbm),
        scratch_shapes=[pltpu.VMEM(x.shape, x.dtype) for x in (fields, *staged)]
        + [
            pltpu.VMEM((3, levels, ny, nx), F32),
            pltpu.VMEM((levels, ny, nx), F32),
            pltpu.VMEM((ny, nx), F32),
            pltpu.VMEM((2, ny, nx), F32),
            pltpu.VMEM((2, 2, ny, nx), F32),
            pltpu.VMEM((2, ny, nx), F32),
            pltpu.VMEM((2, ny, nx), F32),
            pltpu.VMEM((2 * levels, FRINGE, ny), F32),
            pltpu.VMEM((2 * levels, FRINGE, ny), F32),
            pltpu.VMEM((levels, *plane), F32),
            pltpu.VMEM((levels, *plane), F32),
            pltpu.VMEM((levels, *plane), F32),
            pltpu.VMEM((levels, *plane), F32),
            pltpu.VMEM((nb, nb), BF16),
            pltpu.VMEM((nb, nb), BF16),
            pltpu.VMEM((nb, nb), BF16),
            pltpu.VMEM((nb, nb), BF16),
            pltpu.VMEM((nb, nx), F32),
            dma((1 + len(staged),)),
            dma((2 + levels,)),
            dma((3, 2)),
            dma((3, 2)),
            dma((max(groups - 1, 1),)),
            dma,
            dma,
            dma,
            dma((levels,)),
            dma((levels,)),
            dma((levels,)),
            dma((levels,)),
        ],
        compiler_params=pltpu.CompilerParams(
            collective_id=0, has_side_effects=True, vmem_limit_bytes=58 * 1024 * 1024
        ),
        name="fractional_step",
    )(fields, fringe_start, *staged)
    derivs = [tab[4:] for tab in tabs]
    updated, pressure = pl.pallas_call(
        correct,
        out_shape=(
            jax.ShapeDtypeStruct((3, levels, ny, nx), F32),
            jax.ShapeDtypeStruct((levels, ny, nx), F32),
        ),
        in_specs=[hbm] * 4,
        out_specs=(hbm, hbm),
        scratch_shapes=[
            pltpu.VMEM((3, levels, ny, nx), F32),
            pltpu.VMEM((levels + 1, ny, nx), F32),
            pltpu.VMEM((2, ny, ny), BF16),
            pltpu.VMEM((2, nx, nx), BF16),
            dma((levels + 6,)),
            dma((levels + 1,)),
        ],
        compiler_params=pltpu.CompilerParams(vmem_limit_bytes=58 * 1024 * 1024),
        name="correction",
    )(base, planes, derivs[0], derivs[-1])
    return updated[None], pressure[None]


def solution(mesh):
    return jax.shard_map(
        functools.partial(local, mesh.shape["gz"], mesh.shape["group"]),
        mesh=mesh,
        in_specs=(P("group", None, "gz", None, None), P(), P(), P(), P(), P(), P(), P()),
        out_specs=(P("group", None, "gz", None, None), P("group", "gz", None, None)),
        check_vma=False,
    )
```

```python
import functools

import jax
import jax.numpy as jnp
import numpy as np
from jax import lax
from jax.experimental import pallas as pl
from jax.experimental.pallas import tpu as pltpu
from jax.sharding import PartitionSpec as P

FRINGE = 32
TIME_STEP = 0.25
MESH = pl.DeviceIdType.MESH
F32 = jnp.float32
BF16 = jnp.bfloat16


def tables(length):
    ids = np.arange(length)
    middle = length // 2
    wave = np.where(ids <= middle, ids, ids - middle)
    phases = 2.0 * np.pi / length * ((wave[:, None] * ids[None, :]) % length)
    norm = np.sqrt(np.where((ids == 0) | (ids == middle), 1.0, 2.0) / length)[:, None]
    basis = np.where(ids[:, None] <= middle, np.cos(phases), np.sin(phases)) * norm
    coupling = np.zeros((length, length))
    inner = np.arange(1, middle)
    coupling[inner, inner + middle] = 2.0 * np.pi * inner / length
    coupling[inner + middle, inner] = -2.0 * np.pi * inner / length
    deriv = basis.T @ coupling @ basis
    deriv = 0.5 * (deriv - deriv.T)
    parts = []
    for matrix in (basis, basis.T, deriv):
        whole = matrix.astype(np.float32)
        high = whole.astype(jnp.bfloat16)
        parts += [high, (whole - high.astype(np.float32)).astype(jnp.bfloat16)]
    return np.stack(parts)


def split(value):
    high = value.astype(BF16)
    return high, (value - high.astype(F32)).astype(BF16)


def dot(left, right):
    return jnp.dot(left, right, preferred_element_type=F32)


def dot_nt(left, right):
    return lax.dot_general(left, right, (((1,), (1,)), ((), ())), preferred_element_type=F32)


def left_mul(high, low, value):
    vh, vl = split(value)
    return dot(jnp.concatenate([high, high, low], 1), jnp.concatenate([vh, vl, vh], 0))


def right_mul(value, high, low):
    vh, vl = split(value)
    return dot(jnp.concatenate([vh, vl, vh], 1), jnp.concatenate([high, high, low], 0))


def iota(shape, dim):
    return lax.broadcasted_iota(jnp.int32, shape, dim)


def onehot(hit):
    return jnp.where(hit, 1.0, 0.0).astype(BF16)


def kernel(
    n, groups, tab_count,
    vel_hbm, start_ref, *refs,
):
    staged = refs[: 7 + tab_count]
    upd_hbm, prs_hbm = refs[7 + tab_count : 9 + tab_count]
    vel = refs[9 + tab_count]
    local_refs = refs[10 + tab_count : 17 + 2 * tab_count]
    tlevel, trow, tcol, thrust, green, shift, ramp_tab = local_refs[:7]
    tab_y, tab_x = local_refs[7], local_refs[-1]
    (
        upd, prs, p_above, w_side, uv_side, h_src, h_side, fr_src, fr_buf,
        spec, modes, back, planes, m_hi, m_lo, mt_hi, mt_lo, inv,
        in_sem, out_sem, halo_send, halo_recv, fr_send, fr_recv, pa_send, pa_recv,
        x_send, x_recv, y_send, y_recv,
    ) = refs[17 + 2 * tab_count :]
    levels, ny, nx = vel.shape[1:]
    rows = ny // n
    nz = levels * n
    nb = nz * rows
    me = lax.axis_index("gz")
    group = lax.axis_index("group")
    up = lax.rem(me + 1, n)
    down = lax.rem(me + n - 1, n)
    top = levels - 1

    loads = [
        pltpu.make_async_copy(src, dst, in_sem.at[i])
        for i, (src, dst) in enumerate(zip((vel_hbm, *staged), (vel, *local_refs)))
    ]
    loads[0].start()
    barrier = pltpu.get_barrier_semaphore()

    @pl.loop(1, n)
    def _(off):
        pl.semaphore_signal(
            barrier, inc=1, device_id={"gz": lax.rem(me + off, n)}, device_id_type=MESH
        )

    for off in range(1, groups):
        pl.semaphore_signal(
            barrier, inc=1, device_id={"group": lax.rem(group + off, groups)}, device_id_type=MESH
        )
    for load in loads[1:]:
        load.start()
    loads[0].wait()
    pl.semaphore_wait(barrier, n - 1 + groups - 1)

    def remote(src, dst, send, recv, where):
        return pltpu.make_async_remote_copy(
            src_ref=src, dst_ref=dst, send_sem=send, recv_sem=recv,
            device_id=where, device_id_type=MESH,
        )

    inner = 1 - lax.rem(me, 2)
    outer = 1 - inner

    def there(side):
        return jnp.where(side == 1, me < n - 1, me > 0)

    def toward(side):
        return jnp.where(side == 1, up, down)

    uv = pl.ds(0, 2)

    def halo(src, dst, kind, side):
        return remote(
            src, dst.at[1 - side], halo_send.at[kind, side], halo_recv.at[kind, 1 - side],
            {"gz": toward(side)},
        )

    def halo_copy(kind, side):
        if kind == 0:
            return halo(vel.at[2, side * top], w_side, kind, side)
        if kind == 1:
            return halo(h_src.at[side], h_side, kind, side)
        return halo(vel.at[uv, side * top], uv_side, kind, side)

    def send(kind, side):
        @pl.when(there(side))
        def _():
            halo_copy(kind, side).start()

    def receive(kind, side):
        @pl.when(there(side))
        def _():
            halo_copy(kind, 1 - side).wait_recv()

    send(0, inner)
    send(0, outer)

    for side in range(2):

        @pl.when(jnp.logical_not(there(side)))
        def _():
            w_side[side] = jnp.zeros((ny, nx), F32)
            h_side[side] = jnp.zeros((ny, nx), F32)
            uv_side[side] = jnp.zeros((2, ny, nx), F32)

    for load in loads[1:]:
        load.wait()

    start = start_ref[0]
    pick = iota((FRINGE, nx), 1) - start == iota((FRINGE, nx), 0)
    pick_b = onehot(pick)
    fringe_copies = [
        remote(fr_src, fr_buf, fr_send.at[g - 1], fr_recv, {"group": g}) for g in range(1, groups)
    ]

    @pl.when(group == 0)
    def _():
        fr_buf[...] = jnp.zeros_like(fr_buf)
        for c in range(2):
            for k in range(levels):
                vh, vl = split(vel[c, k])
                fr_src[c * levels + k] = dot_nt(pick_b, vh) + dot_nt(pick_b, vl)
        for copy in fringe_copies:
            copy.start()

    is_farm = jnp.where(group > 0, 1.0, 0.0)
    ramp = is_farm * jnp.sum(jnp.where(pick, ramp_tab[...], 0.0), axis=0, keepdims=True)
    keep = 1.0 - ramp

    r_y = (tab_y[0], tab_y[1])
    rt_y = (tab_y[2], tab_y[3])
    d_y = (tab_y[4], tab_y[5])
    r_x = (tab_x[0], tab_x[1])
    rt_x = (tab_x[2], tab_x[3])
    d_x = (tab_x[4], tab_x[5])

    def dx(value):
        return -right_mul(value, *d_x)

    def dy(value):
        return left_mul(*d_y, value)

    turbines = trow.shape[1]
    pick_row = iota((ny, turbines), 0) == trow[...]
    pick_col = onehot(iota((nx, turbines), 0) == tcol[...])

    def predict(c, k):
        field = vel[c, k]
        if k < top and k > 0:
            vertical = vel[c, k + 1] - vel[c, k - 1]
        elif k < top:
            vertical = vel[c, k + 1]
        elif k > 0:
            vertical = -vel[c, k - 1]
        else:
            vertical = jnp.zeros_like(field)
        tend = -(vel[0, k] * dx(field) + vel[1, k] * dy(field) + (0.5 * vel[2, k]) * vertical)
        upd[c, k] = field + TIME_STEP * tend

    for k in range(levels):
        for c in (2, 0, 1):
            predict(c, k)

    half = 0.5 * TIME_STEP

    for side in (inner, outer):
        signed = half * (2 * side - 1).astype(F32)
        edge = side * top
        receive(0, side)
        w_there = w_side[side]
        upd[2, edge] = upd[2, edge] - signed * (vel[2, edge] * w_there)
        weight = (signed * keep) * w_there
        h_src[side] = (
            dx(weight * vel[0, edge])
            + dy(weight * vel[1, edge])
            - side.astype(F32) * upd[2, top]
        )
        send(1, side)

    speed = jnp.zeros((1, turbines), F32)
    for k in range(levels):
        vh, vl = split(vel[0, k])
        at_col = dot(vh, pick_col) + dot(vl, pick_col)
        here = jnp.sum(jnp.where(pick_row, at_col, 0.0), axis=0, keepdims=True)
        speed = speed + jnp.where(tlevel[...] == me * levels + k, here, 0.0)
    drag = (-TIME_STEP * is_farm) * thrust[...] * jnp.abs(speed) * speed
    for k in range(levels):
        placed = jnp.where(pick_row & (tlevel[...] == me * levels + k), drag, 0.0)
        ph, pw = split(placed)
        upd[0, k] = upd[0, k] + dot_nt(ph, pick_col) + dot_nt(pw, pick_col)

    @pl.when(group > 0)
    def _():
        fringe_copies[0].wait_recv()

    for k in range(levels):
        for c in range(2):
            th, tl = split(fr_buf[c * levels + k].T)
            upstream = dot(th, pick_b) + dot(tl, pick_b)
            predicted = upd[c, k]
            upd[c, k] = predicted + ramp * (upstream - predicted)

    for k in range(levels):
        divergence = dx(upd[0, k]) + dy(upd[1, k]) + upd[2, k]
        if k > 0:
            divergence = divergence - upd[2, k - 1]
        prs[k] = divergence

    def exchange(src, dst, send, recv):
        pltpu.make_async_copy(src.at[me], dst.at[me], recv).start()

        @pl.loop(1, n)
        def _(off):
            peer = lax.rem(me + off, n)
            remote(src.at[peer], dst.at[me], send, recv, {"gz": peer}).start()

    def arrived(dst, recv):
        pltpu.make_async_copy(dst, dst, recv).wait()

    def sent(src, send):
        most = src.at[pl.ds(0, n - 1)]
        pltpu.make_async_copy(most, most, send).wait()

    def transform(k):
        put(spec.at[k], right_mul(left_mul(*r_y, prs[k]), *rt_x), n)
        exchange(spec.at[k], modes.at[k], x_send.at[k], x_recv.at[k])

    for side in (inner, outer):
        edge = side * top
        receive(1, side)
        prs[edge] = prs[edge] + h_side[side]
        transform(edge)
    for k in range(1, top):
        transform(k)
    send(2, 1)

    rbits = rows.bit_length() - 1
    ybits = ny.bit_length() - 1
    eig = iota((nb, nz), 0) >> rbits == iota((nb, nz), 1)
    pos = iota((nb, nz), 0)
    lev = ((pos & (ny - 1)) >> rbits) * levels + (pos >> ybits) == iota((nb, nz), 1)
    eig_b, lev_b = onehot(eig), onehot(lev)
    same = (iota((nb, nb), 0) & (rows - 1)) == (iota((nb, nb), 1) & (rows - 1))
    for part, to, to_t in zip(split(green[...]), (m_hi, m_lo), (mt_hi, mt_lo)):
        wide = dot(eig_b, part).astype(BF16)
        to[...] = jnp.where(same, dot_nt(wide, lev_b), 0.0).astype(BF16)
        wide_t = dot_nt(lev_b, part).astype(BF16)
        to_t[...] = jnp.where(same, dot_nt(wide_t, eig_b), 0.0).astype(BF16)
    shifts = jnp.sum(jnp.where(eig, shift[...], 0.0), axis=1, keepdims=True)

    def wave_square(ids, length):
        wave = jnp.where(ids <= length // 2, ids, ids - length // 2)
        wave = wave.astype(F32) * (2.0 * np.pi / length)
        return wave * wave

    ky = me * rows + (iota((nb, 1), 0) & (rows - 1))
    kx = iota((1, nx), 1)
    inv[...] = 1.0 / (shifts + (wave_square(ky, ny) + wave_square(kx, nx)))

    scaled = None
    for k in range(top, -1, -1):
        arrived(modes.at[k], x_recv.at[k])
        cols = pl.ds(k * ny, ny)
        term = left_mul(m_hi[:, cols], m_lo[:, cols], get(modes.at[k]))
        scaled = term if scaled is None else scaled + term
    send(2, 0)
    scaled = scaled * inv[...]
    for k in range(levels):
        own = pl.ds(k * ny, ny)
        put(back.at[k], left_mul(mt_hi[own], mt_lo[own], scaled), n)
        exchange(back.at[k], planes.at[k], y_send.at[k], y_recv.at[k])
    for side in range(2):
        edge = side * top
        signed = half * (2 * side - 1)
        receive(2, side)
        for c in range(2):
            upd[c, edge] = upd[c, edge] - (signed * keep) * (vel[2, edge] * uv_side[side, c])
    out_upd = pltpu.make_async_copy(upd, upd_hbm, out_sem.at[0])
    out_upd.start()

    p_down = remote(prs.at[0], p_above, pa_send, pa_recv, {"gz": down})

    @pl.when(jnp.logical_not(there(1)))
    def _():
        p_above[...] = jnp.zeros((ny, nx), F32)

    out_prs = []
    for k in range(levels):
        arrived(planes.at[k], y_recv.at[k])
        prs[k] = right_mul(left_mul(*rt_y, get(planes.at[k])), *r_x)
        if k == 0:

            @pl.when(there(0))
            def _():
                p_down.start()

        copy = pltpu.make_async_copy(prs.at[k], prs_hbm.at[k], out_sem.at[2 + k])
        copy.start()
        out_prs.append(copy)

    @pl.when(there(1))
    def _():
        p_down.wait_recv()

    out_above = pltpu.make_async_copy(p_above, prs_hbm.at[levels], out_sem.at[1])
    out_above.start()
    out_upd.wait()
    for copy in out_prs:
        copy.wait()
    out_above.wait()

    for side in range(2):

        @pl.when(there(side))
        def _():
            for kind in range(3):
                halo_copy(kind, side).wait_send()

    @pl.when(there(0))
    def _():
        p_down.wait_send()

    @pl.when(group == 0)
    def _():
        for copy in fringe_copies:
            copy.wait_send()

    for k in range(levels):
        sent(spec.at[k], x_send.at[k])
        sent(back.at[k], y_send.at[k])


def correct(base_hbm, planes_hbm, dy_hbm, dx_hbm, upd_hbm, prs_hbm, upd, prs, d_y, d_x, sem, out_sem):
    levels = prs_hbm.shape[0]
    loads = [
        pltpu.make_async_copy(src, dst, sem.at[i])
        for i, (src, dst) in enumerate(
            [(planes_hbm.at[k], prs.at[k]) for k in range(levels)]
            + [
                (dx_hbm, d_x),
                (dy_hbm, d_y),
                (base_hbm.at[pl.ds(0, 2)], upd.at[pl.ds(0, 2)]),
                (planes_hbm.at[levels], prs.at[levels]),
                (base_hbm.at[2], upd.at[2]),
            ]
        )
    ]
    for load in loads:
        load.start()
    for load in loads[: levels + 3]:
        load.wait()
    whole = pltpu.make_async_copy(prs.at[pl.ds(0, levels)], prs_hbm, out_sem.at[levels])
    whole.start()
    outs = []
    uv = pl.ds(0, 2)
    for k in range(levels):
        pressure = prs[k]
        upd[0, k] = upd[0, k] + right_mul(pressure, d_x[0], d_x[1])
        upd[1, k] = upd[1, k] - left_mul(d_y[0], d_y[1], pressure)
        outs.append(pltpu.make_async_copy(upd.at[uv, k], upd_hbm.at[uv, k], out_sem.at[k]))
        outs[-1].start()
    for load in loads[levels + 3 :]:
        load.wait()
    for k in range(levels):
        upd[2, k] = upd[2, k] - (prs[k + 1] - prs[k])
    last = pltpu.make_async_copy(upd.at[2], upd_hbm.at[2], sem.at[levels + 5])
    last.start()
    for copy in (whole, *outs, last):
        copy.wait()


def put(ref, value, n):
    rows = ref.shape[1]
    if rows % 8 == 0:
        ref[...] = value.reshape(ref.shape)
    else:
        for i in range(n):
            ref[i] = value[i * rows : (i + 1) * rows]


def get(ref):
    n, rows, nx = ref.shape
    if rows % 8 == 0:
        return ref[...].reshape(n * rows, nx)
    return jnp.concatenate([ref[i] for i in range(n)], 0)


def local(
    n, groups,
    velocity, fringe_start, turbine_level, turbine_row, turbine_col, thrust, green_basis,
    eigen_shift,
):
    _, _, levels, ny, nx = velocity.shape
    rows = ny // n
    nz = levels * n
    nb = nz * rows
    offset = (np.arange(FRINGE) + 0.5)[:, None]
    ramp_tab = (np.sin(np.pi * offset / FRINGE) ** 2).astype(np.float32)
    hbm = pl.BlockSpec(memory_space=pltpu.HBM)
    smem = pl.BlockSpec(memory_space=pltpu.SMEM)
    plane = (n, rows, nx)
    dma = pltpu.SemaphoreType.DMA
    tabs = [tables(length) for length in ((ny,) if ny == nx else (ny, nx))]
    staged = [
        turbine_level[None], turbine_row[None], turbine_col[None], thrust[None],
        green_basis, eigen_shift[None], ramp_tab, *tabs,
    ]
    fields = velocity[0]
    base, planes = pl.pallas_call(
        functools.partial(kernel, n, groups, len(tabs)),
        out_shape=(
            jax.ShapeDtypeStruct((3, levels, ny, nx), F32),
            jax.ShapeDtypeStruct((levels + 1, ny, nx), F32),
        ),
        in_specs=[hbm, smem] + [hbm] * len(staged),
        out_specs=(hbm, hbm),
        scratch_shapes=[pltpu.VMEM(x.shape, x.dtype) for x in (fields, *staged)]
        + [
            pltpu.VMEM((3, levels, ny, nx), F32),
            pltpu.VMEM((levels, ny, nx), F32),
            pltpu.VMEM((ny, nx), F32),
            pltpu.VMEM((2, ny, nx), F32),
            pltpu.VMEM((2, 2, ny, nx), F32),
            pltpu.VMEM((2, ny, nx), F32),
            pltpu.VMEM((2, ny, nx), F32),
            pltpu.VMEM((2 * levels, FRINGE, ny), F32),
            pltpu.VMEM((2 * levels, FRINGE, ny), F32),
            pltpu.VMEM((levels, *plane), F32),
            pltpu.VMEM((levels, *plane), F32),
            pltpu.VMEM((levels, *plane), F32),
            pltpu.VMEM((levels, *plane), F32),
            pltpu.VMEM((nb, nb), BF16),
            pltpu.VMEM((nb, nb), BF16),
            pltpu.VMEM((nb, nb), BF16),
            pltpu.VMEM((nb, nb), BF16),
            pltpu.VMEM((nb, nx), F32),
            dma((1 + len(staged),)),
            dma((2 + levels,)),
            dma((3, 2)),
            dma((3, 2)),
            dma((max(groups - 1, 1),)),
            dma,
            dma,
            dma,
            dma((levels,)),
            dma((levels,)),
            dma((levels,)),
            dma((levels,)),
        ],
        compiler_params=pltpu.CompilerParams(
            collective_id=0, has_side_effects=True, vmem_limit_bytes=58 * 1024 * 1024
        ),
        name="fractional_step",
    )(fields, fringe_start, *staged)
    derivs = [tab[4:] for tab in tabs]
    updated, pressure = pl.pallas_call(
        correct,
        out_shape=(
            jax.ShapeDtypeStruct((3, levels, ny, nx), F32),
            jax.ShapeDtypeStruct((levels, ny, nx), F32),
        ),
        in_specs=[hbm] * 4,
        out_specs=(hbm, hbm),
        scratch_shapes=[
            pltpu.VMEM((3, levels, ny, nx), F32),
            pltpu.VMEM((levels + 1, ny, nx), F32),
            pltpu.VMEM((2, ny, ny), BF16),
            pltpu.VMEM((2, nx, nx), BF16),
            dma((levels + 6,)),
            dma((levels + 1,)),
        ],
        compiler_params=pltpu.CompilerParams(vmem_limit_bytes=58 * 1024 * 1024),
        name="correction",
    )(base, planes, derivs[0], derivs[-1])
    return updated[None], pressure[None]


def solution(mesh):
    return jax.shard_map(
        functools.partial(local, mesh.shape["gz"], mesh.shape["group"]),
        mesh=mesh,
        in_specs=(P("group", None, "gz", None, None), P(), P(), P(), P(), P(), P(), P()),
        out_specs=(P("group", None, "gz", None, None), P("group", "gz", None, None)),
        check_vma=False,
    )
```
